128 devices in a mesh: row: 8 (over z, x_lo), col: 16 (over x_hi, y, core).
Axes of the slice: x: 4 (x_hi: 2, x_lo: 2; x = x_hi * 2 + x_lo), y: 4, z: 4, core: 2. Of those that a mesh axis runs over, the one named last changes fastest.
Arguments:
- atom_feats: bfloat16 [20480, 128], P(('row', 'col')), may hold values from -6 to 6
- atom_counts: int32 [2048], replicated, may hold values from 1 to 24, as said below
- w_atom: bfloat16 [128, 768], replicated, may hold values from -0.5 to 0.5
- single_in: bfloat16 [2048, 768], P(('row', 'col')), may hold values from -6 to 6
- w_qkv: bfloat16 [3, 768, 768], P(None, None, 'col'), may hold values from -0.21875 to 0.21875
- w_out: bfloat16 [768, 768], P('col'), may hold values from -0.21875 to 0.21875
- pair: bfloat16 [2048, 2048, 128], P('row', 'col'), may hold values from -6 to 6
- w_pair: bfloat16 [128, 16], replicated, may hold values from -0.5 to 0.5
- cotangent: bfloat16 [2048, 768], P(('row', 'col')), may hold values from -192 to 192
Outputs:
- updated: bfloat16 [2048, 768], P(('row', 'col'))
- grad_pair: bfloat16 [2048, 2048, 128], P('row', 'col')
- grad_pair_weight: float32 [128, 16], replicated
The draws below stay inside these ranges and needn't reach their ends.
Inputs may be any that keep to these rules, and one draw needn't show every extreme that they name: `atom_counts`: atoms of one token are consecutive, tokens in order. Each aligned block of 256 tokens holds exactly 2560 atoms; its first 112 tokens have 19 to 24 atoms, one of them 24, and its last 144 tokens are small-molecule tokens of one atom.
All inputs are finite; a program needn't handle non-finite values.
Results may differ from the reference program's by a relative error of at most 0.025.
Values may be sent and summed in bfloat16 or wider, within the bound.
A program may use at most 64 MiB of HBM per device.

```python
import jax
import jax.numpy as jnp
from jax import lax

D = 768
HEADS = 16
HD = 48
CP = 128
CA = 128
TOK_ROW = 256
TOKENS = 2048
ATOMS = 20480
N_ROW = 8


def draw_atom_counts(key, part):
    key = jax.random.fold_in(key, 11)
    blocks = TOKENS // TOK_ROW
    ligand = TOK_ROW // 2 + TOK_ROW // 16
    protein = TOK_ROW - ligand
    rest = protein - 1
    target = 10 * TOK_ROW - ligand - 24
    key_base, key_rank = jax.random.split(key, 2)
    base = jax.random.randint(key_base, (blocks, protein), 20, 23).astype(jnp.int32)
    ranks = jax.vmap(lambda k: jax.random.permutation(k, protein))(jax.random.split(key_rank, blocks)).astype(jnp.int32)
    others = ranks > 0
    summed = jnp.sum(jnp.where(others, base, 0), axis=1).astype(jnp.int32)
    missing = (target - summed).astype(jnp.int32)
    whole = jnp.floor_divide(missing, rest).astype(jnp.int32)
    leftover = (missing - whole * rest).astype(jnp.int32)
    extra = (ranks - 1 < leftover[:, None]).astype(jnp.int32)
    fixed = base + whole[:, None] + extra
    protein_counts = jnp.where(others, fixed, 24).astype(jnp.int32)
    single_atom = jnp.ones((blocks, ligand), jnp.int32)
    return jnp.concatenate([protein_counts, single_atom], axis=1).reshape(TOKENS).astype(jnp.int32)


def block_scale(key, shape, pieces, smallest, largest):
    factor_of = 1.0
    for dim, shards_of in pieces:
        steps = jax.random.uniform(jax.random.fold_in(jax.random.fold_in(key, 6), dim), (shards_of,), jnp.float32, smallest / len(pieces), largest / len(pieces))
        factor_of = factor_of * jnp.repeat(jnp.exp(steps), shape[dim] // shards_of).reshape((-1,) + (1,) * (len(shape) - 1 - dim))
    return factor_of


def noise(stream_key, shape, scale, reach, cuts=(), kind=jnp.bfloat16):
    result = jax.random.normal(stream_key, shape, jnp.float32) * scale
    if len(cuts) > 0:
        result = block_scale(stream_key, shape, cuts, -0.22, 0.18) * result
    return jnp.clip(result, min=-reach, max=reach).astype(kind)


def setup_inputs(seed: int = 0) -> dict:
    streams_of = jax.random.split(jax.random.key(seed), 10)
    return {
        "atom_feats": noise(streams_of[0], (ATOMS, CA), 1.0, 6.0, ((0, 128),)),
        "atom_counts": draw_atom_counts(jax.random.fold_in(streams_of[9], 71), 0),
        "w_atom": noise(streams_of[2], (CA, D), CA ** -0.5, 0.5),
        "single_in": noise(streams_of[3], (TOKENS, D), 1.0, 6.0, ((0, 128),)),
        "w_qkv": noise(streams_of[4], (3, D, D), D ** -0.5, 0.21875, ((2, 16),)),
        "w_out": noise(streams_of[5], (D, D), D ** -0.5, 0.21875, ((0, 16),)),
        "pair": noise(streams_of[6], (TOKENS, TOKENS, CP), 1.0, 6.0, ((0, 8), (1, 16))),
        "w_pair": noise(streams_of[7], (CP, HEADS), CP ** -0.5, 0.5),
        "cotangent": noise(streams_of[8], (TOKENS, D), 32.0, 192.0, ((0, 128),)),
    }


def reference(atom_feats, atom_counts, w_atom, single_in, w_qkv, w_out, pair, w_pair, cotangent):
    ends_at = jnp.cumsum(atom_counts).astype(jnp.int32)
    atom_ids = jnp.arange(ATOMS, dtype=jnp.int32)
    token_of = jnp.searchsorted(ends_at, atom_ids, side='right').astype(jnp.int32)
    atom_hidden = jax.nn.relu(jnp.dot(atom_feats, w_atom, preferred_element_type=jnp.float32)).astype(jnp.bfloat16)
    pooled = jax.ops.segment_sum(atom_hidden.astype(jnp.float32), token_of, TOKENS)
    pooled = pooled / atom_counts.astype(jnp.float32)[:, None]
    single = (single_in.astype(jnp.float32) + pooled).astype(jnp.bfloat16)
    values32 = single.astype(jnp.float32)
    center = lax.optimization_barrier(jnp.mean(values32, axis=1, keepdims=True))
    spread = lax.optimization_barrier(jnp.mean((values32 - center) ** 2, axis=1, keepdims=True))
    normed = ((values32 - center) / jnp.sqrt(spread + 1e-05)).astype(jnp.bfloat16)
    queries = jnp.dot(normed, w_qkv[0], preferred_element_type=jnp.float32).astype(jnp.bfloat16)
    keys = jnp.dot(normed, w_qkv[1], preferred_element_type=jnp.float32).astype(jnp.bfloat16)
    values = jnp.dot(normed, w_qkv[2], preferred_element_type=jnp.float32).astype(jnp.bfloat16)
    pair_blocks = pair.reshape(N_ROW, TOK_ROW, TOKENS, CP)
    wp32 = w_pair.astype(jnp.float32)

    def bias_block(block):
        return jnp.einsum('ijc,ch->hij', block.astype(jnp.float32), wp32).astype(jnp.bfloat16)
    bias = lax.map(bias_block, pair_blocks)
    bias = jnp.moveaxis(bias, 0, 1).reshape(HEADS, TOKENS, TOKENS)
    d_attended = lax.dot_general(cotangent, w_out, (((1,), (1,)), ((), ())), preferred_element_type=jnp.float32).astype(jnp.bfloat16)

    def per_head(items):
        q_h, k_h, v_h, b_h, g_h = items
        scores = jnp.dot(q_h, k_h.T, preferred_element_type=jnp.float32) / jnp.sqrt(jnp.float32(HD))
        scores = scores + b_h.astype(jnp.float32)
        top = lax.optimization_barrier(jnp.max(scores, axis=1, keepdims=True))
        expd = jnp.exp(scores - top)
        probs = expd / lax.optimization_barrier(jnp.sum(expd, axis=1, keepdims=True))
        att = jnp.dot(probs.astype(jnp.bfloat16), v_h, preferred_element_type=jnp.float32).astype(jnp.bfloat16)
        d_probs = jnp.dot(g_h, v_h.T, preferred_element_type=jnp.float32)
        inner = lax.optimization_barrier(jnp.sum(probs * d_probs, axis=1, keepdims=True))
        d_bias = (probs * (d_probs - inner)).astype(jnp.bfloat16)
        return (att, d_bias)

    def by_head(matrix):
        return jnp.moveaxis(matrix.reshape(TOKENS, HEADS, HD), 1, 0)
    att_heads, d_bias = lax.map(per_head, (by_head(queries), by_head(keys), by_head(values), bias, by_head(d_attended)))
    attended = jnp.moveaxis(att_heads, 0, 1).reshape(TOKENS, D)
    updated = (single.astype(jnp.float32) + jnp.dot(attended, w_out, preferred_element_type=jnp.float32)).astype(jnp.bfloat16)
    d_blocks = jnp.moveaxis(d_bias.reshape(HEADS, N_ROW, TOK_ROW, TOKENS), 1, 0)

    def grad_block(items):
        block, d_blk = items
        d32 = d_blk.astype(jnp.float32)
        grad = jnp.einsum('hij,ch->ijc', d32, wp32).astype(jnp.bfloat16)
        weight_part = jnp.einsum('ijc,hij->ch', block.astype(jnp.float32), d32)
        return (grad, weight_part)
    grads, weight_parts = lax.map(grad_block, (pair_blocks, d_blocks))
    grad_pair = grads.reshape(TOKENS, TOKENS, CP)
    grad_pair_weight = lax.optimization_barrier(jnp.sum(weight_parts, axis=0))
    return (updated, grad_pair, grad_pair_weight)
```

```python
import functools

import jax
import jax.numpy as jnp
from jax import lax
from jax.experimental import pallas as pl
from jax.experimental.pallas import tpu as pltpu
from jax.sharding import PartitionSpec as P

MESH = pl.DeviceIdType.MESH
BF = jnp.bfloat16
F32 = jnp.float32
NC = 16
NR = 8
HD = 48
D = 768
GT = 16
SCALE = 1.0 / (48.0**0.5)


def nt(a, b):
    return lax.dot_general(a, b, (((1,), (1,)), ((), ())), preferred_element_type=F32)


def nn(a, b):
    return jnp.dot(a, b, preferred_element_type=F32)


def head_tiles():
    return [(h, t) for h in range(NC) for t in range(6) if 48 * h < 128 * t + 128 and 48 * h + 48 > 128 * t]


def spread(rows, mask_ref):
    pairs = set(head_tiles())
    zero = jnp.zeros((GT, 128), BF)
    out = []
    for h in range(NC):
        out.append(
            jnp.concatenate(
                [
                    rows[:, 128 * t : 128 * t + 128] * mask_ref[16 * h : 16 * h + 16, 128 * t : 128 * t + 128]
                    if (h, t) in pairs
                    else zero
                    for t in range(6)
                ],
                axis=1,
            )
        )
    return jnp.concatenate(out, axis=0)


def main_kernel(
    feats, counts, w_atom, single_in, w_qkv, w_out, pair, w_pair, cot,
    d_out, upd_out, wg_out,
    pairv, part, pool_recv, acc, norm_all, cot_all, wo_all, kv_send, kv_all, q_all, da_all,
    wbd, wt, mask, bias, ebuf, dpbuf, st_send, st_recv, fin_all, att_send, att_recv,
    dbuf, dt, wcol, wrow, krow, vrow, qrow, darow, single_v,
    pair_sem, d_sem,
    pool_ss, pool_rs, norm_ss, norm_rs, cot_ss, cot_rs, wo_ss, wo_rs, kv_ss, kv_rs, q_ss, q_rs,
    da_ss, da_rs, st_ss, st_rs, fin_ss, fin_rs, att_ss, att_rs, wc_ss, wc_rs, wr_ss, wr_rs,
):
    r = lax.axis_index("row")
    c = lax.axis_index("col")

    def loop(lo, hi, body):
        def step(k, carry):
            body(k)
            return carry

        lax.fori_loop(lo, hi, step, 0)

    def pair_copy(g):
        return pltpu.make_async_copy(pair.at[pl.ds(g * GT, GT)], pairv.at[pl.ds(g * GT, GT)], pair_sem.at[g])

    loop(0, 16, lambda g: pair_copy(g).start())

    bar = pltpu.get_barrier_semaphore()
    src_row = c // 2

    def greet_col(k):
        pl.semaphore_signal(bar, inc=1, device_id=(r, lax.rem(c + k, NC)), device_id_type=MESH)

    def greet_row(k):
        pl.semaphore_signal(bar, inc=1, device_id=(lax.rem(r + k, NR), c), device_id_type=MESH)

    def greet_kv(h):
        @pl.when(jnp.logical_or(src_row != r, h != c))
        def _():
            pl.semaphore_signal(bar, inc=1, device_id=(src_row, h), device_id_type=MESH)

    loop(1, NC, greet_col)
    loop(1, NR, greet_row)
    loop(0, NC, greet_kv)

    crow = jnp.concatenate([counts[pl.ds(2 * r, 1), :], counts[pl.ds(2 * r + 1, 1), :]], axis=1).astype(F32)
    tok = lax.broadcasted_iota(jnp.int32, (256, 256), 0)
    lan = lax.broadcasted_iota(jnp.int32, (256, 256), 1)
    cbig = jnp.broadcast_to(crow, (256, 256))
    ends = jnp.sum(jnp.where(lan <= tok, cbig, 0.0), axis=1, keepdims=True)
    cnt = jnp.sum(jnp.where(lan == tok, cbig, 0.0), axis=1, keepdims=True)
    atom = (lan + 160 * c).astype(F32)
    inside = jnp.logical_and(jnp.logical_and(atom < ends, atom >= ends - cnt), lan < 160)
    onehot = jnp.where(inside, 1.0, 0.0).astype(BF)
    x = jnp.concatenate([feats[...], jnp.zeros((96, 128), BF)], axis=0)
    hidden = jnp.maximum(nn(x, w_atom[...]), 0.0).astype(BF)
    part[...] = (nn(onehot, hidden) / cnt).astype(BF).reshape(NC, GT, D)

    row16 = lax.broadcasted_iota(jnp.int32, (16, 256), 0)
    lan16 = lax.broadcasted_iota(jnp.int32, (16, 256), 1)
    rep = jnp.where(lan16 // 16 == row16, 1.0, 0.0).astype(BF)
    wrep = nn(w_pair[...], rep)
    lanw = lax.broadcasted_iota(jnp.int32, (128, 256), 1)
    for i in range(GT):
        wbd[128 * i : 128 * i + 128, :] = jnp.where(lax.rem(lanw, 16) == i, wrep, 0.0).astype(BF)
    eye = jnp.where(
        lax.broadcasted_iota(jnp.int32, (48, 48), 0) == lax.broadcasted_iota(jnp.int32, (48, 48), 1), 1.0, 0.0
    ).astype(BF)
    for m in range(3):
        wt[48 * m : 48 * m + 48, :] = nt(eye, w_qkv[m]).astype(BF)
    mrow = lax.broadcasted_iota(jnp.int32, (256, D), 0)
    mlan = lax.broadcasted_iota(jnp.int32, (256, D), 1)
    mask[...] = jnp.where(mlan // 48 == mrow // 16, 1.0, 0.0).astype(BF)
    cot_all[c] = cot[...]
    wo_all[c] = w_out[...]

    pl.semaphore_wait(bar, 38 - jnp.where(src_row == r, 1, 0))

    def lo(s):
        return (160 * s) // 384

    def hi(s):
        return jnp.where(s == 15, 15, jnp.minimum(6, (160 * s + 159) // 304))

    def pool_copy(o, s):
        return pltpu.make_async_remote_copy(
            part.at[o], pool_recv.at[s], pool_ss.at[o], pool_rs.at[s], device_id=(r, o), device_id_type=MESH
        )

    def sends_to(s, o):
        return jnp.logical_and(jnp.logical_and(o >= lo(s), o <= hi(s)), o != s)

    def pool_start(o):
        @pl.when(sends_to(c, o))
        def _():
            pool_copy(o, c).start()

    loop(0, NC, pool_start)

    def gather_copy(buf, ss, rs, peer, slot):
        return pltpu.make_async_remote_copy(
            buf.at[slot], buf.at[slot], ss.at[peer], rs.at[slot], device_id=(r, peer), device_id_type=MESH
        )

    def gather_start(buf, ss, rs):
        def body(k):
            gather_copy(buf, ss, rs, lax.rem(c + k, NC), c).start()

        loop(1, NC, body)

    def gather_wait(buf, ss, rs):
        def body(k):
            p = lax.rem(c + NC - k, NC)
            gather_copy(buf, ss, rs, p, p).wait_recv()

        loop(1, NC, body)

    def gather_sent(buf, ss, rs):
        def body(k):
            gather_copy(buf, ss, rs, lax.rem(c + k, NC), c).wait_send()

        loop(1, NC, body)

    gather_start(cot_all, cot_ss, cot_rs)

    def bias_group(g):
        pair_copy(g).wait()
        lhs = jnp.concatenate([pairv[g * GT + i] for i in range(GT)], axis=1)
        bias[g] = nn(lhs, wbd[...])

    loop(0, 4, bias_group)

    acc[...] = single_in[...].astype(F32) + part[c].astype(F32)

    def pool_take(s):
        @pl.when(sends_to(s, c))
        def _():
            pool_copy(c, s).wait_recv()
            acc[...] += pool_recv[s].astype(F32)

    loop(0, NC, pool_take)
    single = acc[...].astype(BF)
    single_v[...] = single
    v32 = single.astype(F32)
    center = jnp.mean(v32, axis=1, keepdims=True)
    diff = v32 - center
    var = jnp.mean(diff * diff, axis=1, keepdims=True)
    norm_all[c] = (diff / jnp.sqrt(var + 1e-05)).astype(BF)
    gather_start(norm_all, norm_ss, norm_rs)

    loop(4, 9, bias_group)

    gather_wait(cot_all, cot_ss, cot_rs)
    da_all[c] = nt(w_out[...], cot_all[...].reshape(256, D)).astype(BF)
    gather_start(da_all, da_ss, da_rs)

    loop(9, 12, bias_group)

    gather_wait(norm_all, norm_ss, norm_rs)
    qkv = nt(wt[...], norm_all[...].reshape(256, D)).astype(BF)
    q_all[c] = qkv[0:48]
    kv_send[0] = qkv[48:144, 0:128]
    kv_send[1] = qkv[48:144, 128:256]
    gather_start(q_all, q_ss, q_rs)

    def kv_copy(n, src, r2):
        return pltpu.make_async_remote_copy(
            kv_send.at[lax.rem(n, 2)],
            kv_all.at[src],
            kv_ss.at[n],
            kv_rs.at[src],
            device_id=(n // 2, 2 * r2 + lax.rem(n, 2)),
            device_id_type=MESH,
        )

    def is_self(n):
        return jnp.logical_and(n // 2 == r, 2 * r + lax.rem(n, 2) == c)

    def kv_start(k):
        n = lax.rem(k + 2 * r, 16)

        @pl.when(jnp.logical_not(is_self(n)))
        def _():
            kv_copy(n, c, r).start()

    loop(0, 16, kv_start)

    @pl.when(src_row == r)
    def _():
        kv_all[c] = kv_send[lax.rem(c, 2)]

    gather_start(wo_all, wo_ss, wo_rs)

    loop(12, 16, bias_group)

    def kv_take(h):
        @pl.when(jnp.logical_or(src_row != r, h != c))
        def _():
            kv_copy(0, h, r).wait_recv()

    loop(0, NC, kv_take)
    krow[...] = jnp.transpose(kv_all[:, 0:48, :].reshape(D, 128))
    vrow[...] = jnp.transpose(kv_all[:, 48:96, :].reshape(D, 128))
    gather_wait(da_all, da_ss, da_rs)
    darow[...] = jnp.transpose(da_all[...].reshape(D, 256)).reshape(NC, GT, D)
    gather_wait(q_all, q_ss, q_rs)
    qrow[...] = jnp.transpose(q_all[...].reshape(D, 256)).reshape(NC, GT, D)

    def st_copy(g, s):
        return pltpu.make_async_remote_copy(
            st_send.at[g], st_recv.at[s], st_ss.at[g], st_rs.at[s], device_id=(r, g), device_id_type=MESH
        )

    def score_group(k):
        g = lax.rem(c + k, NC)
        s = nt(krow[...], spread(qrow[g], mask)) * SCALE + bias[g]
        dp = nt(vrow[...], spread(darow[g], mask))
        m = jnp.max(s, axis=0, keepdims=True)
        e = jnp.exp(s - m)
        ebuf[g] = e
        dpbuf[g] = dp
        l = jnp.sum(e, axis=0, keepdims=True)
        t = jnp.sum(e * dp, axis=0, keepdims=True)
        z = jnp.zeros((2, 128), F32)
        st_send[g] = jnp.concatenate(
            [m[:, :128], m[:, 128:], l[:, :128], l[:, 128:], t[:, :128], t[:, 128:], z], axis=0
        )

        @pl.when(g != c)
        def _():
            st_copy(g, c).start()

    loop(1, NC + 1, score_group)
    st_recv[c] = st_send[c]

    def att_copy(g, s):
        return pltpu.make_async_remote_copy(
            att_send.at[g], att_recv.at[s], att_ss.at[g], att_rs.at[s], device_id=(r, g), device_id_type=MESH
        )

    pairs = head_tiles()

    def att_group(k):
        g = lax.rem(c + k, NC)
        et = jnp.transpose(ebuf[g].astype(BF))
        full = nn(et, vrow[...])
        cols = []
        for t in range(6):
            tot = None
            for h, t2 in pairs:
                if t2 == t:
                    sl = (slice(16 * h, 16 * h + 16), slice(128 * t, 128 * t + 128))
                    term = full[sl] * mask[sl].astype(F32)
                    tot = term if tot is None else tot + term
            cols.append(tot)
        att_send[g] = jnp.concatenate(cols, axis=1).astype(BF)

    loop(1, NC + 1, att_group)

    def st_take(k):
        s = lax.rem(c + NC - k, NC)
        st_copy(c, s).wait_recv()

    loop(1, NC, st_take)
    sr = st_recv[...]
    top = jnp.max(sr[:, 0:2, :], axis=0)
    fac = jnp.exp(sr[:, 0:2, :] - top[None])
    tot_l = jnp.sum(fac * sr[:, 2:4, :], axis=0)
    tot_t = jnp.sum(fac * sr[:, 4:6, :], axis=0)
    inv = 1.0 / tot_l
    fin_all[c] = jnp.concatenate([top, inv, tot_t * inv, jnp.zeros((2, 128), F32)], axis=0)
    gather_start(fin_all, fin_ss, fin_rs)

    def att_start(k):
        g = lax.rem(c + k, NC)
        att_copy(g, c).start()

    loop(1, NC, att_start)
    att_recv[c] = att_send[c]

    frow = fac * inv[None]
    fwide = jnp.concatenate([frow[:, 0, :], frow[:, 1, :]], axis=1)
    fbig = jnp.broadcast_to(fwide[:, None, :], (16, 16, 256))
    keep = lax.rem(lax.broadcasted_iota(jnp.int32, (16, 16, 256), 2), 16) == lax.broadcasted_iota(
        jnp.int32, (16, 16, 256), 1
    )
    fbig = jnp.where(keep, fbig, 0.0).reshape(256, 256)
    f_hi = fbig.astype(BF)
    f_lo = (fbig - f_hi.astype(F32)).astype(BF)
    f_all = (nn(f_hi, mask[...]) + nn(f_lo, mask[...])).reshape(16, 16, D)

    gather_wait(fin_all, fin_ss, fin_rs)

    def d_copy(g):
        return pltpu.make_async_copy(dbuf.at[g], d_out.at[g], d_sem.at[g])

    def d_group(g):
        fin = fin_all[g]
        own = st_send[g]
        scale = jnp.exp(own[0:2] - fin[0:2]) * fin[2:4]
        scale = jnp.concatenate([scale[0:1], scale[1:2]], axis=1)
        inner = jnp.concatenate([fin[4:5], fin[5:6]], axis=1)
        d = ((ebuf[g] * scale) * (dpbuf[g] - inner)).astype(BF)
        dbuf[g] = d
        dt[g] = jnp.transpose(d)
        d_copy(g).start()

    loop(0, 16, d_group)

    lhs_w = jnp.concatenate([dt[g] for g in range(NC)], axis=1)
    ii = lax.broadcasted_iota(jnp.int32, (16, 16, 128), 1)
    wcol[c] = jnp.zeros((16, 128), F32)

    def weight_step(n):
        rhs = jnp.concatenate(
            [jnp.concatenate([pairv[g * GT + 2 * n], pairv[g * GT + 2 * n + 1]], axis=1) for g in range(NC)], axis=0
        )
        full = nn(lhs_w, rhs).reshape(16, 16, 256)
        one = jnp.where(ii == 2 * n, full[:, :, 0:128], 0.0) + jnp.where(ii == 2 * n + 1, full[:, :, 128:256], 0.0)
        wcol[c] = wcol[c] + jnp.sum(one, axis=1)

    loop(0, 8, weight_step)
    gather_start(wcol, wc_ss, wc_rs)

    def att_take(k):
        s = lax.rem(c + NC - k, NC)
        att_copy(c, s).wait_recv()

    loop(1, NC, att_take)
    att = jnp.sum(att_recv[...].astype(F32) * f_all, axis=0).astype(BF)
    gather_wait(wo_all, wo_ss, wo_rs)
    proj = nn(att, wo_all[...].reshape(D, D))
    upd_out[...] = (single_v[...].astype(F32) + proj).astype(BF)

    gather_wait(wcol, wc_ss, wc_rs)
    wrow[r] = jnp.sum(wcol[...], axis=0)

    def wr_copy(peer, slot):
        return pltpu.make_async_remote_copy(
            wrow.at[slot], wrow.at[slot], wr_ss.at[peer], wr_rs.at[slot], device_id=(peer, c), device_id_type=MESH
        )

    loop(1, NR, lambda k: wr_copy(lax.rem(r + k, NR), r).start())

    def pool_sent(o):
        @pl.when(sends_to(c, o))
        def _():
            pool_copy(o, c).wait_send()

    loop(0, NC, pool_sent)
    gather_sent(cot_all, cot_ss, cot_rs)
    gather_sent(norm_all, norm_ss, norm_rs)
    gather_sent(da_all, da_ss, da_rs)
    gather_sent(q_all, q_ss, q_rs)
    gather_sent(wo_all, wo_ss, wo_rs)
    gather_sent(fin_all, fin_ss, fin_rs)
    gather_sent(wcol, wc_ss, wc_rs)

    def kv_sent(n):
        @pl.when(jnp.logical_not(is_self(n)))
        def _():
            kv_copy(n, c, r).wait_send()

    loop(0, 16, kv_sent)

    def st_sent(k):
        g = lax.rem(c + k, NC)
        st_copy(g, c).wait_send()
        att_copy(g, c).wait_send()

    loop(1, NC, st_sent)
    loop(0, 16, lambda g: d_copy(g).wait())

    def wr_take(k):
        p = lax.rem(r + NR - k, NR)
        wr_copy(p, p).wait_recv()

    loop(1, NR, wr_take)
    loop(1, NR, lambda k: wr_copy(lax.rem(r + k, NR), r).wait_send())
    wg_out[...] = jnp.sum(wrow[...], axis=0)


def grad_kernel(d, w_pair, upd, wg, upd_out, grad, wg_out, w2, out, sem):
    upd_out[...] = upd[...]
    wide = jnp.concatenate([wg[...], jnp.zeros((112, 128), F32)], axis=0)
    wg_out[...] = jnp.transpose(wide)[:, 0:16]
    rowi = lax.broadcasted_iota(jnp.int32, (256, 16), 0)
    lani = lax.broadcasted_iota(jnp.int32, (256, 16), 1)
    rep = jnp.where(rowi // 16 == lani, 1.0, 0.0).astype(BF)
    wrep = nt(rep, w_pair[...])
    rowm = lax.rem(lax.broadcasted_iota(jnp.int32, (256, 128), 0), 16)
    for i in range(GT):
        w2[:, 128 * i : 128 * i + 128] = jnp.where(rowm == i, wrep, 0.0).astype(BF)

    def copy(g):
        return pltpu.make_async_copy(out.at[pl.ds(g * GT, GT)], grad.at[pl.ds(g * GT, GT)], sem.at[g])

    def step(g, carry):
        full = nn(d[g], w2[...]).astype(BF)
        for i in range(GT):
            out[g * GT + i] = full[:, 128 * i : 128 * i + 128]
        copy(g).start()
        return carry

    lax.fori_loop(0, 16, step, 0)

    def done(g, carry):
        copy(g).wait()
        return carry

    lax.fori_loop(0, 16, done, 0)


def on_device(atom_feats, atom_counts, w_atom, single_in, w_qkv, w_out, pair, w_pair, cotangent):
    vm = pl.BlockSpec(memory_space=pltpu.VMEM)
    hbm = pl.BlockSpec(memory_space=pl.ANY)
    V = pltpu.VMEM
    dma = pltpu.SemaphoreType.DMA
    sems16 = dma((16,))
    d_bias, upd, wg = pl.pallas_call(
        main_kernel,
        name="attend",
        out_shape=(
            jax.ShapeDtypeStruct((16, 128, 256), BF),
            jax.ShapeDtypeStruct((16, D), BF),
            jax.ShapeDtypeStruct((16, 128), F32),
        ),
        in_specs=[vm, vm, vm, vm, vm, vm, hbm, vm, vm],
        out_specs=(hbm, vm, vm),
        scratch_shapes=[
            V((256, 128, 128), BF),
            V((16, 16, D), BF),
            V((16, 16, D), BF),
            V((16, D), F32),
            V((16, 16, D), BF),
            V((16, 16, D), BF),
            V((16, 48, D), BF),
            V((2, 96, 128), BF),
            V((16, 96, 128), BF),
            V((16, 48, 256), BF),
            V((16, 48, 256), BF),
            V((2048, 256), BF),
            V((144, D), BF),
            V((256, D), BF),
            V((16, 128, 256), F32),
            V((16, 128, 256), F32),
            V((16, 128, 256), F32),
            V((16, 8, 128), F32),
            V((16, 8, 128), F32),
            V((16, 8, 128), F32),
            V((16, 16, D), BF),
            V((16, 16, D), BF),
            V((16, 128, 256), BF),
            V((16, 256, 128), BF),
            V((16, 16, 128), F32),
            V((8, 16, 128), F32),
            V((128, D), BF),
            V((128, D), BF),
            V((16, 16, D), BF),
            V((16, 16, D), BF),
            V((16, D), BF),
            sems16,
            sems16,
        ]
        + [sems16] * 22
        + [dma((8,))] * 2,
        compiler_params=pltpu.CompilerParams(collective_id=0, has_side_effects=True, vmem_limit_bytes=56 << 20),
    )(
        atom_feats,
        atom_counts.reshape(16, 128),
        w_atom,
        single_in,
        w_qkv,
        w_out,
        pair,
        w_pair,
        cotangent,
    )
    updated, grad_pair, grad_w = pl.pallas_call(
        grad_kernel,
        name="grad_pair",
        out_shape=(
            jax.ShapeDtypeStruct((16, D), BF),
            jax.ShapeDtypeStruct((256, 128, 128), BF),
            jax.ShapeDtypeStruct((128, 16), F32),
        ),
        in_specs=[vm, vm, vm, vm],
        out_specs=(vm, hbm, vm),
        scratch_shapes=[V((256, 2048), BF), V((256, 128, 128), BF), sems16],
        compiler_params=pltpu.CompilerParams(vmem_limit_bytes=48 << 20),
    )(d_bias, w_pair, upd, wg)
    return updated, grad_pair, grad_w


def solution(mesh):
    placed = (
        P(("row", "col"), None),
        P(),
        P(),
        P(("row", "col"), None),
        P(None, None, "col"),
        P("col", None),
        P("row", "col", None),
        P(),
        P(("row", "col"), None),
    )
    return jax.shard_map(
        on_device,
        mesh=mesh,
        in_specs=placed,
        out_specs=(P(("row", "col"), None), P("row", "col", None), P()),
        check_vma=False,
    )
```

```python
import jax
import jax.numpy as jnp
from jax import lax
from jax.experimental import pallas as pl
from jax.experimental.pallas import tpu as pltpu
from jax.sharding import PartitionSpec as P

MESH = pl.DeviceIdType.MESH
BF = jnp.bfloat16
F32 = jnp.float32
NC = 16
NR = 8
HD = 48
HP = 64
D = 768
DP = NC * HP
GT = 16
SCALE = 1.0 / (48.0**0.5)


def nt(a, b):
    return lax.dot_general(a, b, (((1,), (1,)), ((), ())), preferred_element_type=F32)


def nn(a, b):
    return jnp.dot(a, b, preferred_element_type=F32)


def loop(lo, hi, body):
    def step(k, carry):
        body(k)
        return carry

    lax.fori_loop(lo, hi, step, 0)


def iota(shape, dim):
    return lax.broadcasted_iota(jnp.int32, shape, dim)


def to_row(col):
    eye = iota((128, 128), 0) == iota((128, 128), 1)
    return [
        jnp.sum(jnp.where(eye, col[128 * n : 128 * n + 128], 0.0), axis=0, keepdims=True)
        for n in range(2)
    ]


def lane_sum(x):
    return jnp.broadcast_to(jnp.sum(x, axis=1, keepdims=True), x.shape)


def to_col(rows):
    eye = iota((128, 128), 0) == iota((128, 128), 1)
    return lane_sum(
        jnp.concatenate([jnp.where(eye, jnp.broadcast_to(rows[n : n + 1], (128, 128)), 0.0) for n in range(2)], axis=0)
    )


def main_kernel(
    feats, counts, w_atom, single_in, w_qkv, w_out, pair, w_pair, cot,
    d_out, upd_out, wg_out,
    pairv, feats_v, counts_v, w_atom_v, single_in_v, wt, wp_v,
    part, pool_recv, acc, norm_all, cot_all, wo_all, kv_row, kv_all, q_all, da_all,
    wbd, maskp, bias, sbuf, dpbuf, eb, st_send, st_recv, fin_all, att_send, att_recv,
    dbuf, dt, wcol, wrow, vrow, qrow, darow, single_v, upd_v, wg_v,
    in_sem, pair_sem, d_sem, out_sem,
    pool_ss, pool_rs, norm_ss, norm_rs, cot_ss, cot_rs, wo_ss, wo_rs, kv_ss, kv_rs, q_ss, q_rs,
    da_ss, da_rs, st_ss, st_rs, fin_ss, fin_rs, att_ss, att_rs, wc_ss, wc_rs, kvr_ss, kvr_rs, wr_ss, wr_rs,
):
    r = lax.axis_index("row")
    c = lax.axis_index("col")
    chip = c // 2
    core = lax.rem(c, 2)
    mate = 2 * chip + 1 - core

    ins = [
        pltpu.make_async_copy(a, b, in_sem.at[n])
        for n, (a, b) in enumerate(
            [
                (feats, feats_v.at[pl.ds(0, 160)]),
                (counts, counts_v),
                (w_atom, w_atom_v),
                (w_pair, wp_v),
                (cot, cot_all.at[c]),
                (single_in, single_in_v),
                (w_out, wo_all.at[c, pl.ds(0, HD)]),
                (w_qkv, wt),
            ]
        )
    ]
    for cp in ins:
        cp.start()

    def pair_copy(g):
        return pltpu.make_async_copy(pair.at[pl.ds(g * GT, GT)], pairv.at[pl.ds(g * GT, GT)], pair_sem.at[g])

    loop(0, 16, lambda g: pair_copy(g).start())

    bar = pltpu.get_barrier_semaphore()

    def greet_col(k):
        pl.semaphore_signal(bar, inc=1, device_id=(r, lax.rem(c + k, NC)), device_id_type=MESH)

    def greet_row(k):
        pl.semaphore_signal(bar, inc=1, device_id=(lax.rem(r + k, NR), c), device_id_type=MESH)

    loop(1, NC, greet_col)
    loop(1, NR, greet_row)

    feats_v[160:256, :] = jnp.zeros((96, 128), BF)
    ins[1].wait()
    crow = jnp.concatenate([counts_v[pl.ds(2 * r, 1), :], counts_v[pl.ds(2 * r + 1, 1), :]], axis=1).astype(F32)
    tok = iota((256, 256), 0)
    lan = iota((256, 256), 1)
    cbig = jnp.broadcast_to(crow, (256, 256))
    ends = jnp.sum(jnp.where(lan <= tok, cbig, 0.0), axis=1, keepdims=True)
    cnt = jnp.sum(jnp.where(lan == tok, cbig, 0.0), axis=1, keepdims=True)
    atom = (lan + 160 * c).astype(F32)
    inside = jnp.logical_and(jnp.logical_and(atom < ends, atom >= ends - cnt), lan < 160)
    onehot = jnp.where(inside, 1.0, 0.0).astype(BF)
    ins[0].wait()
    ins[2].wait()
    hidden = jnp.maximum(nn(feats_v[...], w_atom_v[...]), 0.0).astype(BF)
    part[...] = (nn(onehot, hidden) / cnt).astype(BF).reshape(NC, GT, D)

    ins[3].wait()
    rep = jnp.where(iota((256, 16), 0) // 16 == iota((256, 16), 1), 1.0, 0.0).astype(BF)
    wrep = lax.dot_general(wp_v[...], rep, (((0,), (1,)), ((), ())), preferred_element_type=F32)
    lanw = lax.rem(iota((128, 256), 1), 16)
    for i in range(GT):
        wbd[128 * i : 128 * i + 128, :] = jnp.where(lanw == i, wrep, 0.0).astype(BF)
    maskp[...] = jnp.where(iota((256, DP), 1) // HP == iota((256, DP), 0) // GT, 1.0, 0.0).astype(BF)
    pad = jnp.zeros((NC, HP - HD, 256), BF)
    q_all[:, HD:HP, :] = pad
    da_all[:, HD:HP, :] = pad
    kv_all[:, 0, HD:HP, :] = pad[:, :, 0:128]
    kv_all[:, 1, HD:HP, :] = pad[:, :, 0:128]
    wo_all[:, HD:HP, :] = jnp.zeros((NC, HP - HD, D), BF)
    for n in range(4, 8):
        ins[n].wait()

    pl.semaphore_wait(bar, 22)

    def lo(s):
        return (160 * s) // 384

    def hi(s):
        return jnp.where(s == 15, 15, jnp.minimum(6, (160 * s + 159) // 304))

    def pool_copy(o, s):
        return pltpu.make_async_remote_copy(
            part.at[o], pool_recv.at[s], pool_ss.at[o], pool_rs.at[s], device_id=(r, o), device_id_type=MESH
        )

    def sends_to(s, o):
        return jnp.logical_and(jnp.logical_and(o >= lo(s), o <= hi(s)), o != s)

    def pool_start(o):
        @pl.when(sends_to(c, o))
        def _():
            pool_copy(o, c).start()

    loop(0, NC, pool_start)

    def piece(buf, slot, rows):
        return buf.at[slot] if rows is None else buf.at[slot, pl.ds(0, rows)]

    def gather_copy(buf, rows, ss, rs, peer, slot, n):
        return pltpu.make_async_remote_copy(
            piece(buf, slot, rows), piece(buf, slot, rows), ss.at[n], rs.at[slot], device_id=(r, peer), device_id_type=MESH
        )

    def near(k):
        return 2 * lax.rem(chip + k, 8) + core

    def gather_start(buf, rows, ss, rs):
        gather_copy(buf, rows, ss, rs, mate, c, 0).start()
        loop(1, 8, lambda k: gather_copy(buf, rows, ss, rs, near(k), c, k).start())

    def gather_relay(buf, rows, ss, rs):
        def body(k):
            slot = near(8 - k)
            gather_copy(buf, rows, ss, rs, slot, slot, k).wait_recv()
            gather_copy(buf, rows, ss, rs, mate, slot, 8 + k).start()

        loop(1, 8, body)

    def gather_end(buf, rows, ss, rs):
        def body(k):
            slot = 2 * lax.rem(chip + 8 - k, 8) + 1 - core
            gather_copy(buf, rows, ss, rs, mate, slot, 0).wait_recv()

        loop(0, 8, body)

    def gather_sent(buf, rows, ss, rs):
        def body(k):
            gather_copy(buf, rows, ss, rs, near(k), c, k).wait_send()
            gather_copy(buf, rows, ss, rs, mate, c, 8 + k).wait_send()

        gather_copy(buf, rows, ss, rs, mate, c, 0).wait_send()
        loop(1, 8, body)

    g_cot = (cot_all, None, cot_ss, cot_rs)
    g_norm = (norm_all, None, norm_ss, norm_rs)
    g_da = (da_all, HD, da_ss, da_rs)
    g_q = (q_all, HD, q_ss, q_rs)
    g_wo = (wo_all, HD, wo_ss, wo_rs)

    gather_start(*g_cot)

    def bias_group(g):
        pair_copy(g).wait()
        lhs = jnp.concatenate([pairv[g * GT + i] for i in range(GT)], axis=1)
        bias[g] = jnp.transpose(nn(lhs, wbd[...]).astype(BF))

    loop(0, 3, bias_group)

    acc[...] = single_in_v[...].astype(F32) + part[c].astype(F32)

    def pool_take(s):
        @pl.when(sends_to(s, c))
        def _():
            pool_copy(c, s).wait_recv()
            acc[...] += pool_recv[s].astype(F32)

    loop(0, NC, pool_take)
    single = acc[...].astype(BF)
    single_v[...] = single
    v32 = single.astype(F32)
    center = jnp.mean(v32, axis=1, keepdims=True)
    diff = v32 - center
    var = jnp.mean(diff * diff, axis=1, keepdims=True)
    norm_all[c] = (diff / jnp.sqrt(var + 1e-05)).astype(BF)
    gather_start(*g_norm)

    gather_relay(*g_cot)
    loop(3, 6, bias_group)
    gather_end(*g_cot)
    da_all[c, 0:HD] = nt(wo_all[c, 0:HD], cot_all[...].reshape(256, D)).astype(BF)
    gather_start(*g_da)

    loop(6, 10, bias_group)

    gather_relay(*g_norm)
    gather_end(*g_norm)
    qkv = nt(wt[...].reshape(3 * HD, D), norm_all[...].reshape(256, D)).astype(BF)
    q_all[c, 0:HD] = qkv[0:HD]
    for half in range(2):
        for n in range(2):
            kv_row[r, half, n] = qkv[HD * (n + 1) : HD * (n + 2), 128 * half : 128 * half + 128]

    def kvr_copy(peer, slot):
        return pltpu.make_async_remote_copy(
            kv_row.at[slot], kv_row.at[slot], kvr_ss.at[peer], kvr_rs.at[slot], device_id=(peer, c), device_id_type=MESH
        )

    loop(1, NR, lambda k: kvr_copy(lax.rem(r + k, NR), r).start())
    gather_start(*g_q)

    def kv_copy(b, half, s):
        return pltpu.make_async_remote_copy(
            kv_row.at[b, half],
            kv_all.at[s, :, pl.ds(0, HD)],
            kv_ss.at[2 * b + half],
            kv_rs.at[s],
            device_id=(r, 2 * b + half),
            device_id_type=MESH,
        )

    def kv_forward(b):
        for half in range(2):
            @pl.when(2 * b + half != c)
            def _(half=half):
                kv_copy(b, half, c).start()

            @pl.when(2 * b + half == c)
            def _(half=half):
                kv_all[c, :, 0:HD, :] = kv_row[b, half]

    kv_forward(r)
    gather_relay(*g_da)
    loop(10, 12, bias_group)

    def kvr_take(k):
        b = lax.rem(r + NR - k, NR)
        kvr_copy(b, b).wait_recv()
        kv_forward(b)

    loop(1, NR, kvr_take)
    gather_relay(*g_q)
    loop(12, 16, bias_group)

    gather_end(*g_da)
    dat = jnp.transpose(da_all[...].reshape(DP, 256))
    for m in range(4):
        darow[m] = dat[:, 256 * m : 256 * m + 256].reshape(NC, GT, 256)
    gather_end(*g_q)
    qt = jnp.transpose(q_all[...].reshape(DP, 256))
    for m in range(4):
        qrow[m] = qt[:, 256 * m : 256 * m + 256].reshape(NC, GT, 256)

    def kv_take(h):
        @pl.when(h != c)
        def _():
            kv_copy(0, 0, h).wait_recv()

    loop(0, NC, kv_take)

    lan128 = iota((16, 128), 1)
    first = jnp.where(lan128 < HP, 1.0, 0.0).astype(BF)
    second = jnp.where(lan128 >= HP, 1.0, 0.0).astype(BF)
    none = jnp.zeros((16, 128), BF)

    def spread(rows_ref, m):
        out = []
        for g in range(NC):
            a, b = rows_ref[m, g, :, 0:128], rows_ref[m, g, :, 128:256]
            out += [
                jnp.concatenate([a * first, none], axis=1),
                jnp.concatenate([a * second, none], axis=1),
                jnp.concatenate([none, b * first], axis=1),
                jnp.concatenate([none, b * second], axis=1),
            ]
        return jnp.concatenate(out, axis=0)

    def quad(m):
        kt = kv_all[4 * m : 4 * m + 4, 0].reshape(4 * HP, 128)
        vt = kv_all[4 * m : 4 * m + 4, 1].reshape(4 * HP, 128)
        sbuf[m] = nn(spread(qrow, m), kt).reshape(NC, 64, 128)
        dpbuf[m] = nn(spread(darow, m), vt).reshape(NC, 64, 128)
        vrow[2 * m] = jnp.transpose(vt[0:128])
        vrow[2 * m + 1] = jnp.transpose(vt[128:256])

    for m in range(4):
        quad(m)
    gather_start(*g_wo)

    def st_copy(g, s):
        return pltpu.make_async_remote_copy(
            st_send.at[g], st_recv.at[s], st_ss.at[g], st_rs.at[s], device_id=(r, g), device_id_type=MESH
        )

    U = 4

    def soft_step(q):
        gs = [U * q + u for u in range(U)]
        s = jnp.concatenate([sbuf[m, g] for g in gs for m in range(4)], axis=0)
        b = jnp.concatenate([bias[g] for g in gs], axis=0)
        dp = jnp.concatenate([dpbuf[m, g] for g in gs for m in range(4)], axis=0)
        s = s * SCALE + b.astype(F32)
        top = jnp.max(s, axis=1, keepdims=True)
        e = jnp.exp(s - top)
        l = lane_sum(e)
        t = lane_sum(e * dp)
        e16 = e.astype(BF)
        top = jnp.broadcast_to(top, e.shape)
        stats = []
        for u in range(U):
            part_of = slice(256 * u, 256 * u + 256)
            rows = to_row(top[part_of]) + to_row(l[part_of]) + to_row(t[part_of]) + [jnp.zeros((2, 128), F32)]
            stats.append(jnp.concatenate(rows, axis=0))
        for u, g in enumerate(gs):
            for m in range(4):
                k = 256 * u + 64 * m
                sbuf[m, g] = e[k : k + 64]
                eb[m, g] = e16[k : k + 64]
            st_send[g] = stats[u]
        for g in gs:
            @pl.when(g != c)
            def _(g=g):
                st_copy(g, c).start()

    loop(0, NC // U, soft_step)
    st_recv[c] = st_send[c]

    def att_copy(g, s):
        return pltpu.make_async_remote_copy(
            att_send.at[g], att_recv.at[s], att_ss.at[g], att_rs.at[s], device_id=(r, g), device_id_type=MESH
        )

    keep = iota((16, 16, 128), 2) < HP
    for p in range(8):
        rows = eb[p // 2, :, 32 * (p % 2) : 32 * (p % 2) + 32, :].reshape(512, 128)
        full = nn(rows, vrow[p]).reshape(NC, 2, GT, 128)
        att_send[:, :, 128 * p : 128 * p + 128] = jnp.where(keep, full[:, 0], full[:, 1]).astype(BF)

    loop(1, NC, lambda k: st_copy(c, lax.rem(c + NC - k, NC)).wait_recv())
    sr = st_recv[...]
    best = jnp.max(sr[:, 0:2, :], axis=0)
    fac = jnp.exp(sr[:, 0:2, :] - best[None])
    tot_l = jnp.sum(fac * sr[:, 2:4, :], axis=0)
    tot_t = jnp.sum(fac * sr[:, 4:6, :], axis=0)
    inv = 1.0 / tot_l
    fin_all[c] = jnp.concatenate([best, inv, tot_t * inv, jnp.zeros((2, 128), F32)], axis=0)

    def fin_copy(peer, slot):
        return pltpu.make_async_remote_copy(
            fin_all.at[slot], fin_all.at[slot], fin_ss.at[peer], fin_rs.at[slot], device_id=(r, peer), device_id_type=MESH
        )

    loop(1, NC, lambda k: fin_copy(lax.rem(c + k, NC), c).start())
    loop(1, NC, lambda k: att_copy(lax.rem(c + k, NC), c).start())
    att_recv[c] = att_send[c]

    frow = fac * inv[None]
    fwide = jnp.concatenate([frow[:, 0, :], frow[:, 1, :]], axis=1)
    fbig = jnp.broadcast_to(fwide[:, None, :], (16, 16, 256))
    diag = lax.rem(iota((16, 16, 256), 2), 16) == iota((16, 16, 256), 1)
    fbig = jnp.where(diag, fbig, 0.0).reshape(256, 256)
    f_hi = fbig.astype(BF)
    f_lo = (fbig - f_hi.astype(F32)).astype(BF)
    f_all = (nn(f_hi, maskp[...]) + nn(f_lo, maskp[...])).reshape(16, 16, DP)
    gather_relay(*g_wo)

    def d_copy(g):
        return pltpu.make_async_copy(dt.at[g], d_out.at[g], d_sem.at[g])

    loop(1, NC, lambda k: fin_copy(c, lax.rem(c + NC - k, NC)).wait_recv())

    W = 8

    def d_step(q):
        gs = [W * q + u for u in range(W)]
        scale, inner = [], []
        for g in gs:
            fin, own = fin_all[g], st_send[g]
            scale.append(to_col(jnp.exp(own[0:2] - fin[0:2]) * fin[2:4]))
            inner.append(to_col(fin[4:6]))
        e = jnp.concatenate([sbuf[m, g] for g in gs for m in range(4)], axis=0)
        dp = jnp.concatenate([dpbuf[m, g] for g in gs for m in range(4)], axis=0)
        d = (e * jnp.concatenate(scale, axis=0)) * (dp - jnp.concatenate(inner, axis=0))
        dbuf[pl.ds(W * q, W)] = d.reshape(W, 256, 128)

    loop(0, NC // W, d_step)

    def weight_step(q):
        lhs = [dbuf[4 * q + n, pl.ds(i, NC, stride=GT), :] for n in range(4) for i in range(GT)]
        rhs = pairv[pl.ds(4 * GT * q, 4 * GT)].reshape(4 * GT * 128, 128)
        return nn(jnp.concatenate(lhs, axis=1).astype(BF), rhs)

    wcol[c] = lax.fori_loop(0, 4, lambda q, tot: tot + weight_step(q), jnp.zeros((16, 128), F32))

    def wc_copy(peer, slot):
        return pltpu.make_async_remote_copy(
            wcol.at[slot], wcol.at[slot], wc_ss.at[peer], wc_rs.at[slot], device_id=(r, peer), device_id_type=MESH
        )

    loop(1, NC, lambda k: wc_copy(lax.rem(c + k, NC), c).start())

    def d_turn(g):
        dt[g] = jnp.transpose(dbuf[g].astype(BF))
        d_copy(g).start()

    loop(0, 16, d_turn)

    loop(1, NC, lambda k: att_copy(c, lax.rem(c + NC - k, NC)).wait_recv())
    att = jnp.sum(att_recv[...].astype(F32) * f_all, axis=0).astype(BF)
    gather_end(*g_wo)
    proj = nn(att, wo_all[...].reshape(DP, D))
    upd_v[...] = (single_v[...].astype(F32) + proj).astype(BF)
    upd_copy = pltpu.make_async_copy(upd_v, upd_out, out_sem.at[0])
    upd_copy.start()

    loop(1, NC, lambda k: wc_copy(c, lax.rem(c + NC - k, NC)).wait_recv())
    wrow[r] = jnp.sum(wcol[...], axis=0)

    def wr_copy(peer, slot):
        return pltpu.make_async_remote_copy(
            wrow.at[slot], wrow.at[slot], wr_ss.at[peer], wr_rs.at[slot], device_id=(peer, c), device_id_type=MESH
        )

    loop(1, NR, lambda k: wr_copy(lax.rem(r + k, NR), r).start())

    def pool_sent(o):
        @pl.when(sends_to(c, o))
        def _():
            pool_copy(o, c).wait_send()

    loop(0, NC, pool_sent)
    for g in (g_cot, g_norm, g_da, g_q, g_wo):
        gather_sent(*g)
    loop(1, NR, lambda k: kvr_copy(lax.rem(r + k, NR), r).wait_send())

    def kv_sent(b):
        for half in range(2):
            @pl.when(2 * b + half != c)
            def _(half=half):
                kv_copy(b, half, c).wait_send()

    loop(0, NR, kv_sent)

    def col_sent(k):
        p = lax.rem(c + k, NC)
        st_copy(p, c).wait_send()
        att_copy(p, c).wait_send()
        fin_copy(p, c).wait_send()
        wc_copy(p, c).wait_send()

    loop(1, NC, col_sent)
    loop(0, 16, lambda g: d_copy(g).wait())
    upd_copy.wait()
    loop(1, NR, lambda k: wr_copy(r, lax.rem(r + NR - k, NR)).wait_recv())
    loop(1, NR, lambda k: wr_copy(lax.rem(r + k, NR), r).wait_send())
    wg_v[...] = jnp.sum(wrow[...], axis=0)
    wg_copy = pltpu.make_async_copy(wg_v, wg_out, out_sem.at[1])
    wg_copy.start()
    wg_copy.wait()


def grad_kernel(d, w_pair, upd, wg, upd_out, grad, wg_out, dv, wp_v, w2, out, in_sem, d_sem, sem):
    small = [
        pltpu.make_async_copy(w_pair, wp_v, in_sem.at[0]),
        pltpu.make_async_copy(upd, upd_out, in_sem.at[1]),
        pltpu.make_async_copy(wg, wg_out, in_sem.at[2]),
    ]
    for cp in small:
        cp.start()

    def d_copy(g):
        return pltpu.make_async_copy(d.at[g], dv.at[g], d_sem.at[g])

    loop(0, 16, lambda g: d_copy(g).start())
    rep = jnp.where(iota((256, 16), 0) // 16 == iota((256, 16), 1), 1.0, 0.0).astype(BF)
    small[0].wait()
    wrep = nn(rep, wp_v[...])
    rowm = lax.rem(iota((256, 128), 0), 16)
    for i in range(GT):
        w2[:, 128 * i : 128 * i + 128] = jnp.where(rowm == i, wrep, 0.0).astype(BF)

    def copy(g):
        return pltpu.make_async_copy(out.at[pl.ds(g * GT, GT)], grad.at[pl.ds(g * GT, GT)], sem.at[g])

    def step(g):
        d_copy(2 * g).wait()
        d_copy(2 * g + 1).wait()
        lhs = dv[pl.ds(2 * g, 2)].reshape(256, 256)
        for n in range(8):
            full = nn(lhs, w2[:, 256 * n : 256 * n + 256]).astype(BF)
            for k in range(2):
                for i in range(2):
                    out[(2 * g + k) * GT + 2 * n + i] = full[128 * k : 128 * k + 128, 128 * i : 128 * i + 128]
        copy(2 * g).start()
        copy(2 * g + 1).start()

    loop(0, 8, step)
    loop(0, 16, lambda g: copy(g).wait())
    small[1].wait()
    small[2].wait()


def on_device(atom_feats, atom_counts, w_atom, single_in, w_qkv, w_out, pair, w_pair, cotangent):
    hbm = pl.BlockSpec(memory_space=pl.ANY)
    V = pltpu.VMEM
    dma = pltpu.SemaphoreType.DMA
    wp = w_pair.T
    d_bias, upd, wg = pl.pallas_call(
        main_kernel,
        name="attend",
        out_shape=(
            jax.ShapeDtypeStruct((16, 128, 256), BF),
            jax.ShapeDtypeStruct((16, D), BF),
            jax.ShapeDtypeStruct((16, 128), F32),
        ),
        in_specs=[hbm] * 9,
        out_specs=(hbm, hbm, hbm),
        scratch_shapes=[
            V((256, 128, 128), BF),
            V((256, 128), BF),
            V((16, 128), jnp.int32),
            V((128, D), BF),
            V((16, D), BF),
            V((3, HD, D), BF),
            V((16, 128), BF),
            V((16, 16, D), BF),
            V((16, 16, D), BF),
            V((16, D), F32),
            V((16, 16, D), BF),
            V((16, 16, D), BF),
            V((16, HP, D), BF),
            V((8, 2, 2, HD, 128), BF),
            V((16, 2, HP, 128), BF),
            V((16, HP, 256), BF),
            V((16, HP, 256), BF),
            V((2048, 256), BF),
            V((256, DP), BF),
            V((16, 256, 128), BF),
            V((4, 16, 64, 128), F32),
            V((4, 16, 64, 128), F32),
            V((4, 16, 64, 128), BF),
            V((16, 8, 128), F32),
            V((16, 8, 128), F32),
            V((16, 8, 128), F32),
            V((16, 16, DP), BF),
            V((16, 16, DP), BF),
            V((16, 256, 128), F32),
            V((16, 128, 256), BF),
            V((16, 16, 128), F32),
            V((8, 16, 128), F32),
            V((8, 128, 128), BF),
            V((4, 16, 16, 256), BF),
            V((4, 16, 16, 256), BF),
            V((16, D), BF),
            V((16, D), BF),
            V((16, 128), F32),
            dma((8,)),
            dma((16,)),
            dma((16,)),
            dma((2,)),
        ]
        + [dma((16,))] * 22
        + [dma((8,))] * 4,
        compiler_params=pltpu.CompilerParams(collective_id=0, has_side_effects=True, vmem_limit_bytes=56 << 20),
    )(
        atom_feats,
        atom_counts.reshape(16, 128),
        w_atom,
        single_in,
        jnp.swapaxes(w_qkv, 1, 2),
        w_out,
        pair,
        wp,
        cotangent,
    )
    updated, grad_pair, grad_w = pl.pallas_call(
        grad_kernel,
        name="grad_pair",
        out_shape=(
            jax.ShapeDtypeStruct((16, D), BF),
            jax.ShapeDtypeStruct((256, 128, 128), BF),
            jax.ShapeDtypeStruct((16, 128), F32),
        ),
        in_specs=[hbm] * 4,
        out_specs=(hbm, hbm, hbm),
        scratch_shapes=[
            V((16, 128, 256), BF),
            V((16, 128), BF),
            V((256, 2048), BF),
            V((256, 128, 128), BF),
            dma((3,)),
            dma((16,)),
            dma((16,)),
        ],
        compiler_params=pltpu.CompilerParams(vmem_limit_bytes=60 << 20),
    )(d_bias, wp, upd, wg)
    return updated, grad_pair, grad_w.T


def solution(mesh):
    placed = (
        P(("row", "col"), None),
        P(),
        P(),
        P(("row", "col"), None),
        P(None, None, "col"),
        P("col", None),
        P("row", "col", None),
        P(),
        P(("row", "col"), None),
    )
    return jax.shard_map(
        on_device,
        mesh=mesh,
        in_specs=placed,
        out_specs=(P(("row", "col"), None), P("row", "col", None), P()),
        check_vma=False,
    )
```

```python
import jax
import jax.numpy as jnp
from jax import lax
from jax.experimental import pallas as pl
from jax.experimental.pallas import tpu as pltpu
from jax.sharding import PartitionSpec as P

MESH = pl.DeviceIdType.MESH
BF = jnp.bfloat16
F32 = jnp.float32
NC = 16
NR = 8
HD = 48
HP = 64
D = 768
DP = NC * HP
GT = 16
SCALE = 1.0 / (48.0**0.5)


def nt(a, b):
    return lax.dot_general(a, b, (((1,), (1,)), ((), ())), preferred_element_type=F32)


def nn(a, b):
    return jnp.dot(a, b, preferred_element_type=F32)


def loop(lo, hi, body):
    def step(k, carry):
        body(k)
        return carry

    lax.fori_loop(lo, hi, step, 0)


def iota(shape, dim):
    return lax.broadcasted_iota(jnp.int32, shape, dim)


def to_row(col):
    eye = iota((128, 128), 0) == iota((128, 128), 1)
    return [
        jnp.sum(jnp.where(eye, col[128 * n : 128 * n + 128], 0.0), axis=0, keepdims=True)
        for n in range(2)
    ]


def lane_sum(x):
    return jnp.broadcast_to(jnp.sum(x, axis=1, keepdims=True), x.shape)


def to_col(rows):
    eye = iota((128, 128), 0) == iota((128, 128), 1)
    return lane_sum(
        jnp.concatenate([jnp.where(eye, jnp.broadcast_to(rows[n : n + 1], (128, 128)), 0.0) for n in range(2)], axis=0)
    )


def main_kernel(
    feats, counts, w_atom, single_in, w_qkv, w_out, pair, w_pair, cot,
    d_out, upd_out, wg_out,
    pairv, feats_v, counts_v, w_atom_v, single_in_v, wt, wp_v,
    part, pool_recv, acc, norm_all, cot_all, wo_all, kv_row, kv_all, q_all, da_all,
    wbd, maskp, bias, sbuf, dpbuf, eb, st_send, st_recv, st3, mst, cst, fin3, att_send, att_recv,
    dbuf, dt, wcol, wsum, vrow, qrow, darow, single_v, upd_v,
    in_sem, pair_sem, d_sem, out_sem,
    pool_ss, pool_rs, norm_ss, norm_rs, cot_ss, cot_rs, wo_ss, wo_rs, kv_ss, kv_rs, q_ss, q_rs,
    da_ss, da_rs, st_ss, st_rs, att_ss, att_rs, wc_ss, wc_rs, kvr_ss, kvr_rs, wr_ss, wr_rs, cst_ss, cst_rs,
    fin_ss, fin_rs, mst_ss, mst_rs,
):
    r = lax.axis_index("row")
    c = lax.axis_index("col")
    chip = c // 2
    core = lax.rem(c, 2)
    mate = 2 * chip + 1 - core

    ins = [
        pltpu.make_async_copy(a, b, in_sem.at[n])
        for n, (a, b) in enumerate(
            [
                (feats, feats_v.at[pl.ds(0, 160)]),
                (counts, counts_v),
                (w_atom, w_atom_v),
                (w_pair, wp_v),
                (cot, cot_all.at[c]),
                (single_in, single_in_v),
                (w_out, wo_all.at[c, pl.ds(0, HD)]),
                (w_qkv, wt),
            ]
        )
    ]
    for cp in ins:
        cp.start()

    def pair_copy(g):
        return pltpu.make_async_copy(pair.at[pl.ds(g * GT, GT)], pairv.at[pl.ds(g * GT, GT)], pair_sem.at[g])

    loop(0, 16, lambda g: pair_copy(g).start())

    bar = pltpu.get_barrier_semaphore()

    def greet_col(k):
        pl.semaphore_signal(bar, inc=1, device_id=(r, lax.rem(c + k, NC)), device_id_type=MESH)

    def greet_row(k):
        pl.semaphore_signal(bar, inc=1, device_id=(lax.rem(r + k, NR), c), device_id_type=MESH)

    loop(1, NC, greet_col)
    loop(1, NR, greet_row)

    feats_v[160:256, :] = jnp.zeros((96, 128), BF)
    ins[1].wait()
    crow = jnp.concatenate([counts_v[pl.ds(2 * r, 1), :], counts_v[pl.ds(2 * r + 1, 1), :]], axis=1).astype(F32)
    tok = iota((256, 256), 0)
    lan = iota((256, 256), 1)
    cbig = jnp.broadcast_to(crow, (256, 256))
    ends = jnp.sum(jnp.where(lan <= tok, cbig, 0.0), axis=1, keepdims=True)
    cnt = jnp.sum(jnp.where(lan == tok, cbig, 0.0), axis=1, keepdims=True)
    atom = (lan + 160 * c).astype(F32)
    inside = jnp.logical_and(jnp.logical_and(atom < ends, atom >= ends - cnt), lan < 160)
    onehot = jnp.where(inside, 1.0, 0.0).astype(BF)
    ins[0].wait()
    ins[2].wait()
    hidden = jnp.maximum(nn(feats_v[...], w_atom_v[...]), 0.0).astype(BF)
    part[...] = (nn(onehot, hidden) / cnt).astype(BF).reshape(NC, GT, D)

    ins[3].wait()
    rep = jnp.where(iota((256, 16), 0) // 16 == iota((256, 16), 1), 1.0, 0.0).astype(BF)
    wrep = lax.dot_general(wp_v[...], rep, (((0,), (1,)), ((), ())), preferred_element_type=F32)
    lanw = lax.rem(iota((128, 256), 1), 16)
    for i in range(GT):
        wbd[128 * i : 128 * i + 128, :] = jnp.where(lanw == i, wrep, 0.0).astype(BF)
    maskp[...] = jnp.where(iota((256, DP), 1) // HP == iota((256, DP), 0) // GT, 1.0, 0.0).astype(BF)
    pad = jnp.zeros((NC, HP - HD, 256), BF)
    q_all[:, HD:HP, :] = pad
    da_all[:, HD:HP, :] = pad
    kv_all[:, 0, HD:HP, :] = pad[:, :, 0:128]
    kv_all[:, 1, HD:HP, :] = pad[:, :, 0:128]
    st_send[...] = jnp.zeros((NC, 8, 128), F32)
    wo_all[:, HD:HP, :] = jnp.zeros((NC, HP - HD, D), BF)
    for n in range(4, 8):
        ins[n].wait()

    def bias_group(k):
        gs = [2 * k, 2 * k + 1]
        for g in gs:
            pair_copy(g).wait()
        lhs = jnp.concatenate([jnp.concatenate([pairv[g * GT + i] for i in range(GT)], axis=1) for g in gs], axis=0)
        out = nn(lhs, wbd[...]).astype(BF)
        for n, g in enumerate(gs):
            bias[g] = jnp.transpose(out[128 * n : 128 * n + 128])

    loop(0, 1, bias_group)
    pl.semaphore_wait(bar, 22)

    def lo(s):
        return (160 * s) // 384

    def hi(s):
        return jnp.where(s == 15, 15, jnp.minimum(6, (160 * s + 159) // 304))

    def pool_copy(o, s):
        return pltpu.make_async_remote_copy(
            part.at[o], pool_recv.at[s], pool_ss.at[o], pool_rs.at[s], device_id=(r, o), device_id_type=MESH
        )

    def sends_to(s, o):
        return jnp.logical_and(jnp.logical_and(o >= lo(s), o <= hi(s)), o != s)

    def pool_start(o):
        @pl.when(sends_to(c, o))
        def _():
            pool_copy(o, c).start()

    loop(0, NC, pool_start)

    def piece(buf, slot, rows):
        return buf.at[slot] if rows is None else buf.at[slot, pl.ds(0, rows)]

    def gather_copy(buf, rows, ss, rs, peer, slot, n):
        return pltpu.make_async_remote_copy(
            piece(buf, slot, rows), piece(buf, slot, rows), ss.at[n], rs.at[slot], device_id=(r, peer), device_id_type=MESH
        )

    def near(k):
        return 2 * lax.rem(chip + k, 8) + core

    def gather_start(buf, rows, ss, rs):
        gather_copy(buf, rows, ss, rs, mate, c, 0).start()
        loop(1, 8, lambda k: gather_copy(buf, rows, ss, rs, near(k), c, k).start())

    def gather_relay(buf, rows, ss, rs):
        def body(k):
            slot = near(8 - k)
            gather_copy(buf, rows, ss, rs, slot, slot, k).wait_recv()
            gather_copy(buf, rows, ss, rs, mate, slot, 8 + k).start()

        loop(1, 8, body)

    def gather_end(buf, rows, ss, rs):
        def body(k):
            slot = 2 * lax.rem(chip + 8 - k, 8) + 1 - core
            gather_copy(buf, rows, ss, rs, mate, slot, 0).wait_recv()

        loop(0, 8, body)

    def gather_sent(buf, rows, ss, rs):
        def body(k):
            gather_copy(buf, rows, ss, rs, near(k), c, k).wait_send()
            gather_copy(buf, rows, ss, rs, mate, c, 8 + k).wait_send()

        gather_copy(buf, rows, ss, rs, mate, c, 0).wait_send()
        loop(1, 8, body)

    g_cot = (cot_all, None, cot_ss, cot_rs)
    g_norm = (norm_all, None, norm_ss, norm_rs)
    g_da = (da_all, HD, da_ss, da_rs)
    g_q = (q_all, HD, q_ss, q_rs)
    g_wo = (wo_all, HD, wo_ss, wo_rs)

    gather_start(*g_cot)

    loop(1, 3, bias_group)

    acc[...] = single_in_v[...].astype(F32) + part[c].astype(F32)

    def pool_take(s):
        @pl.when(sends_to(s, c))
        def _():
            pool_copy(c, s).wait_recv()
            acc[...] += pool_recv[s].astype(F32)

    loop(0, NC, pool_take)
    single = acc[...].astype(BF)
    single_v[...] = single
    v32 = single.astype(F32)
    center = jnp.mean(v32, axis=1, keepdims=True)
    diff = v32 - center
    var = jnp.mean(diff * diff, axis=1, keepdims=True)
    norm_all[c] = (diff / jnp.sqrt(var + 1e-05)).astype(BF)
    gather_start(*g_norm)

    gather_relay(*g_cot)
    loop(3, 4, bias_group)
    gather_end(*g_cot)
    da_all[c, 0:HD] = nt(wo_all[c, 0:HD], cot_all[...].reshape(256, D)).astype(BF)
    gather_start(*g_da)

    loop(4, 6, bias_group)

    gather_relay(*g_norm)
    gather_end(*g_norm)
    qkv = nt(wt[...].reshape(3 * HD, D), norm_all[...].reshape(256, D)).astype(BF)
    q_all[c, 0:HD] = qkv[0:HD]
    for half in range(2):
        for n in range(2):
            kv_row[r, half, n] = qkv[HD * (n + 1) : HD * (n + 2), 128 * half : 128 * half + 128]

    def kvr_copy(peer, slot, half):
        return pltpu.make_async_remote_copy(
            kv_row.at[slot, half],
            kv_row.at[slot, half],
            kvr_ss.at[2 * peer + half],
            kvr_rs.at[2 * slot + half],
            device_id=(peer, c),
            device_id_type=MESH,
        )

    for half in range(2):
        loop(1, NR, lambda k, half=half: kvr_copy(lax.rem(r + k, NR), r, half).start())
    gather_start(*g_q)

    def kv_copy(b, half, s):
        return pltpu.make_async_remote_copy(
            kv_row.at[b, half],
            kv_all.at[s, :, pl.ds(0, HD)],
            kv_ss.at[2 * b + half],
            kv_rs.at[s],
            device_id=(r, 2 * b + half),
            device_id_type=MESH,
        )

    def kv_forward(b, halves=(0, 1)):
        for half in halves:
            @pl.when(2 * b + half != c)
            def _(half=half):
                kv_copy(b, half, c).start()

            @pl.when(2 * b + half == c)
            def _(half=half):
                kv_all[c, :, 0:HD, :] = kv_row[b, half]

    kv_forward(r)

    def kvr_take(k, half):
        b = lax.rem(r + NR - k, NR)
        kvr_copy(b, b, half).wait_recv()
        kv_forward(b, (half,))

    for half in range(2):
        loop(1, NR, lambda k, half=half: kvr_take(k, half))
    gather_relay(*g_da)
    gather_relay(*g_q)
    loop(6, 8, bias_group)

    lan128 = iota((16, 128), 1)
    first = jnp.where(lan128 < HP, 1.0, 0.0).astype(BF)
    second = jnp.where(lan128 >= HP, 1.0, 0.0).astype(BF)
    none = jnp.zeros((16, 128), BF)

    def spread(rows_ref, m):
        out = []
        for g in range(NC):
            a, b = rows_ref[m, g, :, 0:128], rows_ref[m, g, :, 128:256]
            out += [
                jnp.concatenate([a * first, none], axis=1),
                jnp.concatenate([a * second, none], axis=1),
                jnp.concatenate([none, b * first], axis=1),
                jnp.concatenate([none, b * second], axis=1),
            ]
        return jnp.concatenate(out, axis=0)

    def head_ready(h):
        @pl.when(h != c)
        def _():
            kv_copy(0, 0, h).wait_recv()

        @pl.when(jnp.logical_and(lax.rem(h, 2) != core, h != c))
        def _():
            gather_copy(*g_q, mate, h, 0).wait_recv()
            gather_copy(*g_da, mate, h, 0).wait_recv()

    def quad(m):
        loop(4 * m, 4 * m + 4, head_ready)
        qrow[m] = jnp.transpose(q_all[4 * m : 4 * m + 4].reshape(256, 256)).reshape(NC, GT, 256)
        darow[m] = jnp.transpose(da_all[4 * m : 4 * m + 4].reshape(256, 256)).reshape(NC, GT, 256)
        kt = kv_all[4 * m : 4 * m + 4, 0].reshape(4 * HP, 128)
        vt = kv_all[4 * m : 4 * m + 4, 1].reshape(4 * HP, 128)
        sbuf[m] = nn(spread(qrow, m), kt).reshape(NC, 64, 128)
        dpbuf[m] = nn(spread(darow, m), vt).reshape(NC, 64, 128)
        vrow[2 * m] = jnp.transpose(vt[0:128])
        vrow[2 * m + 1] = jnp.transpose(vt[128:256])

    for m in range(4):
        quad(m)
    gather_start(*g_wo)

    def st_copy(g, s):
        return pltpu.make_async_remote_copy(
            st_send.at[g], st_recv.at[s], st_ss.at[g], st_rs.at[s], device_id=(r, g), device_id_type=MESH
        )

    U = 4

    def soft_step(q):
        gs = [U * q + u for u in range(U)]
        s = jnp.concatenate([sbuf[m, g] for g in gs for m in range(4)], axis=0)
        b = jnp.concatenate([bias[g] for g in gs], axis=0)
        dp = jnp.concatenate([dpbuf[m, g] for g in gs for m in range(4)], axis=0)
        s = s * SCALE + b.astype(F32)
        top = jnp.max(s, axis=1, keepdims=True)
        e = jnp.exp(s - top)
        l = lane_sum(e)
        t = lane_sum(e * dp)
        e16 = e.astype(BF)
        top = jnp.broadcast_to(top, e.shape)
        stats = [
            jnp.concatenate([row for u in range(U) for row in to_row(x[256 * u : 256 * u + 256])], axis=0)
            for x in (top, l, t)
        ]
        for u, g in enumerate(gs):
            for m in range(4):
                k = 256 * u + 64 * m
                sbuf[m, g] = e[k : k + 64]
                eb[m, g] = e16[k : k + 64]
            st_send[g, 0:2] = stats[0][2 * u : 2 * u + 2]
        for n in range(3):
            st3[n, pl.ds(2 * U * q, 2 * U)] = stats[n]

    loop(0, NC // U, soft_step)

    def half_of(ref, k):
        return ref.at[:, pl.ds(16 * k, 16)]

    half_copy = pltpu.make_async_remote_copy(
        half_of(st3, 1 - core), mst, mst_ss, mst_rs, device_id=(r, mate), device_id_type=MESH
    )
    half_copy.start()

    def att_copy(g, s):
        return pltpu.make_async_remote_copy(
            att_send.at[g], att_recv.at[s], att_ss.at[g], att_rs.at[s], device_id=(r, g), device_id_type=MESH
        )

    keep = iota((16, 16, 128), 2) < HP
    for p in range(8):
        rows = eb[p // 2, :, 32 * (p % 2) : 32 * (p % 2) + 32, :].reshape(512, 128)
        full = nn(rows, vrow[p]).reshape(NC, 2, GT, 128)
        att_send[:, :, 128 * p : 128 * p + 128] = jnp.where(keep, full[:, 0], full[:, 1]).astype(BF)

    half_copy.wait_recv()
    sa, sb = st3[:, pl.ds(16 * core, 16)], mst[...]
    top2 = jnp.maximum(sa[0], sb[0])
    fa, fb = jnp.exp(sa[0] - top2), jnp.exp(sb[0] - top2)
    cst[chip, 0] = top2
    cst[chip, 1] = sa[1] * fa + sb[1] * fb
    cst[chip, 2] = sa[2] * fa + sb[2] * fb

    def cst_copy(peer, slot):
        return pltpu.make_async_remote_copy(
            cst.at[slot], cst.at[slot], cst_ss.at[peer], cst_rs.at[slot], device_id=(r, 2 * peer + core), device_id_type=MESH
        )

    loop(1, 8, lambda k: cst_copy(lax.rem(chip + k, 8), chip).start())
    def att_start(k):
        g = lax.rem(c + k, NC)
        st_copy(g, c).start()
        att_copy(g, c).start()

    loop(1, NC, att_start)
    st_recv[c] = st_send[c]
    att_recv[c] = att_send[c]
    loop(1, 8, lambda k: cst_copy(chip, lax.rem(chip + 8 - k, 8)).wait_recv())
    all_st = cst[...]
    best = jnp.max(all_st[:, 0], axis=0)
    fac = jnp.exp(all_st[:, 0] - best[None])
    inv = 1.0 / jnp.sum(fac * all_st[:, 1], axis=0)
    mine = pl.ds(16 * core, 16)
    fin3[0, mine] = best
    fin3[1, mine] = inv
    fin3[2, mine] = jnp.sum(fac * all_st[:, 2], axis=0) * inv

    def fin_copy(k):
        return pltpu.make_async_remote_copy(
            half_of(fin3, k), half_of(fin3, k), fin_ss, fin_rs, device_id=(r, mate), device_id_type=MESH
        )

    fin_copy(core).start()


    def d_copy(g):
        return pltpu.make_async_copy(dt.at[g], d_out.at[g], d_sem.at[g])

    W = 8

    def d_step(n):
        k = lax.rem(core + n, 2)

        @pl.when(n == 1)
        def _():
            fin_copy(1 - core).wait_recv()

        half = pl.ds(16 * k, 16)
        scales = jnp.exp(st3[0, half] - fin3[0, half]) * fin3[1, half]
        inners = fin3[2, half]
        scale = [to_col(scales[2 * u : 2 * u + 2]) for u in range(W)]
        inner = [to_col(inners[2 * u : 2 * u + 2]) for u in range(W)]
        gs = [W * k + u for u in range(W)]
        e = jnp.concatenate([sbuf[m, g] for g in gs for m in range(4)], axis=0)
        dp = jnp.concatenate([dpbuf[m, g] for g in gs for m in range(4)], axis=0)
        d = (e * jnp.concatenate(scale, axis=0)) * (dp - jnp.concatenate(inner, axis=0))
        dbuf[pl.ds(W * k, W)] = d.reshape(W, 256, 128)

    loop(0, 2, d_step)

    def weight_step(q):
        lhs = [dbuf[4 * q + n, pl.ds(i, NC, stride=GT), :] for n in range(4) for i in range(GT)]
        rhs = pairv[pl.ds(4 * GT * q, 4 * GT)].reshape(4 * GT * 128, 128)
        return nn(jnp.concatenate(lhs, axis=1).astype(BF), rhs)

    wcol[c] = lax.fori_loop(0, 4, lambda q, tot: tot + weight_step(q), jnp.zeros((16, 128), F32))

    def wc_copy(peer, slot):
        return pltpu.make_async_remote_copy(
            wcol.at[slot], wcol.at[slot], wc_ss.at[peer], wc_rs.at[slot], device_id=(r, peer), device_id_type=MESH
        )

    loop(1, NC, lambda k: wc_copy(lax.rem(c + k, NC), c).start())

    gather_relay(*g_wo)

    def d_turn(g):
        dt[g] = jnp.transpose(dbuf[g].astype(BF))
        d_copy(g).start()

    loop(0, 16, d_turn)

    loop(1, NC, lambda k: wc_copy(c, lax.rem(c + NC - k, NC)).wait_recv())
    wsum[...] = jnp.sum(wcol[...], axis=0)

    def wr_copy(peer, slot):
        return pltpu.make_async_remote_copy(
            wsum, wg_out.at[slot], wr_ss.at[peer], wr_rs.at[slot], device_id=(peer, c), device_id_type=MESH
        )

    loop(1, NR, lambda k: wr_copy(lax.rem(r + k, NR), r).start())
    wg_copy = pltpu.make_async_copy(wsum, wg_out.at[r], out_sem.at[1])
    wg_copy.start()

    def att_take(k):
        s = lax.rem(c + NC - k, NC)
        st_copy(c, s).wait_recv()
        att_copy(c, s).wait_recv()

    loop(1, NC, att_take)
    here = pl.ds(2 * c, 2)
    frow = jnp.exp(st_recv[:, 0:2, :] - fin3[0, here][None]) * fin3[1, here][None]
    fwide = jnp.concatenate([frow[:, 0, :], frow[:, 1, :]], axis=1)
    fbig = jnp.broadcast_to(fwide[:, None, :], (16, 16, 256))
    diag = lax.rem(iota((16, 16, 256), 2), 16) == iota((16, 16, 256), 1)
    fbig = jnp.where(diag, fbig, 0.0).reshape(256, 256)
    f_hi = fbig.astype(BF)
    f_lo = (fbig - f_hi.astype(F32)).astype(BF)
    f_all = (nn(f_hi, maskp[...]) + nn(f_lo, maskp[...])).reshape(16, 16, DP)
    att = jnp.sum(att_recv[...].astype(F32) * f_all, axis=0).astype(BF)
    gather_end(*g_wo)
    proj = nn(att, wo_all[...].reshape(DP, D))
    upd_v[...] = (single_v[...].astype(F32) + proj).astype(BF)
    upd_copy = pltpu.make_async_copy(upd_v, upd_out, out_sem.at[0])
    upd_copy.start()

    def pool_sent(o):
        @pl.when(sends_to(c, o))
        def _():
            pool_copy(o, c).wait_send()

    loop(0, NC, pool_sent)
    for g in (g_cot, g_norm, g_da, g_q, g_wo):
        gather_sent(*g)
    for half in range(2):
        loop(1, NR, lambda k, half=half: kvr_copy(lax.rem(r + k, NR), r, half).wait_send())

    def kv_sent(b):
        for half in range(2):
            @pl.when(2 * b + half != c)
            def _(half=half):
                kv_copy(b, half, c).wait_send()

    loop(0, NR, kv_sent)

    def col_sent(k):
        p = lax.rem(c + k, NC)
        st_copy(p, c).wait_send()
        att_copy(p, c).wait_send()
        wc_copy(p, c).wait_send()

    loop(1, NC, col_sent)
    half_copy.wait_send()
    fin_copy(core).wait_send()
    loop(1, 8, lambda k: cst_copy(lax.rem(chip + k, 8), chip).wait_send())
    loop(0, 16, lambda g: d_copy(g).wait())
    upd_copy.wait()
    loop(1, NR, lambda k: wr_copy(r, lax.rem(r + NR - k, NR)).wait_recv())
    loop(1, NR, lambda k: wr_copy(lax.rem(r + k, NR), r).wait_send())
    wg_copy.wait()


def grad_kernel(d, w_pair, upd, wg, upd_out, grad, wg_out, dv, wp_v, wr_v, wg_v, w2, out, in_sem, d_sem, sem):
    small = [
        pltpu.make_async_copy(w_pair, wp_v, in_sem.at[0]),
        pltpu.make_async_copy(upd, upd_out, in_sem.at[1]),
        pltpu.make_async_copy(wg, wr_v, in_sem.at[2]),
    ]
    for cp in small:
        cp.start()

    def d_copy(g):
        return pltpu.make_async_copy(d.at[g], dv.at[g], d_sem.at[g])

    loop(0, 16, lambda g: d_copy(g).start())
    rep = jnp.where(iota((256, 16), 0) // 16 == iota((256, 16), 1), 1.0, 0.0).astype(BF)
    small[0].wait()
    wrep = nn(rep, wp_v[...])
    rowm = lax.rem(iota((256, 128), 0), 16)
    for i in range(GT):
        w2[:, 128 * i : 128 * i + 128] = jnp.where(rowm == i, wrep, 0.0).astype(BF)

    def copy(g):
        return pltpu.make_async_copy(out.at[pl.ds(g * GT, GT)], grad.at[pl.ds(g * GT, GT)], sem.at[g])

    def step(g):
        d_copy(2 * g).wait()
        d_copy(2 * g + 1).wait()
        lhs = dv[pl.ds(2 * g, 2)].reshape(256, 256)
        for n in range(8):
            full = nn(lhs, w2[:, 256 * n : 256 * n + 256]).astype(BF)
            for k in range(2):
                for i in range(2):
                    out[(2 * g + k) * GT + 2 * n + i] = full[128 * k : 128 * k + 128, 128 * i : 128 * i + 128]
        copy(2 * g).start()
        copy(2 * g + 1).start()

    loop(0, 8, step)
    small[2].wait()
    wg_v[...] = jnp.sum(wr_v[...], axis=0)
    wg_copy = pltpu.make_async_copy(wg_v, wg_out, in_sem.at[3])
    wg_copy.start()
    loop(0, 16, lambda g: copy(g).wait())
    small[1].wait()
    wg_copy.wait()


def on_device(atom_feats, atom_counts, w_atom, single_in, w_qkv, w_out, pair, w_pair, cotangent):
    hbm = pl.BlockSpec(memory_space=pl.ANY)
    V = pltpu.VMEM
    dma = pltpu.SemaphoreType.DMA
    wp = w_pair.T
    d_bias, upd, wg = pl.pallas_call(
        main_kernel,
        name="attend",
        out_shape=(
            jax.ShapeDtypeStruct((16, 128, 256), BF),
            jax.ShapeDtypeStruct((16, D), BF),
            jax.ShapeDtypeStruct((NR, 16, 128), F32),
        ),
        in_specs=[hbm] * 9,
        out_specs=(hbm, hbm, hbm),
        scratch_shapes=[
            V((256, 128, 128), BF),
            V((256, 128), BF),
            V((16, 128), jnp.int32),
            V((128, D), BF),
            V((16, D), BF),
            V((3, HD, D), BF),
            V((16, 128), BF),
            V((16, 16, D), BF),
            V((16, 16, D), BF),
            V((16, D), F32),
            V((16, 16, D), BF),
            V((16, 16, D), BF),
            V((16, HP, D), BF),
            V((8, 2, 2, HD, 128), BF),
            V((16, 2, HP, 128), BF),
            V((16, HP, 256), BF),
            V((16, HP, 256), BF),
            V((2048, 256), BF),
            V((256, DP), BF),
            V((16, 256, 128), BF),
            V((4, 16, 64, 128), F32),
            V((4, 16, 64, 128), F32),
            V((4, 16, 64, 128), BF),
            V((16, 8, 128), F32),
            V((16, 8, 128), F32),
            V((3, 32, 128), F32),
            V((3, 16, 128), F32),
            V((8, 3, 16, 128), F32),
            V((3, 32, 128), F32),
            V((16, 16, DP), BF),
            V((16, 16, DP), BF),
            V((16, 256, 128), F32),
            V((16, 128, 256), BF),
            V((16, 16, 128), F32),
            V((16, 128), F32),
            V((8, 128, 128), BF),
            V((4, 16, 16, 256), BF),
            V((4, 16, 16, 256), BF),
            V((16, D), BF),
            V((16, D), BF),
            dma((8,)),
            dma((16,)),
            dma((16,)),
            dma((2,)),
        ]
        + [dma((16,))] * 22
        + [dma((8,))] * 4
        + [dma] * 4,
        compiler_params=pltpu.CompilerParams(collective_id=0, has_side_effects=True, vmem_limit_bytes=56 << 20),
    )(
        atom_feats,
        atom_counts.reshape(16, 128),
        w_atom,
        single_in,
        jnp.swapaxes(w_qkv, 1, 2),
        w_out,
        pair,
        wp,
        cotangent,
    )
    updated, grad_pair, grad_w = pl.pallas_call(
        grad_kernel,
        name="grad_pair",
        out_shape=(
            jax.ShapeDtypeStruct((16, D), BF),
            jax.ShapeDtypeStruct((256, 128, 128), BF),
            jax.ShapeDtypeStruct((16, 128), F32),
        ),
        in_specs=[hbm] * 4,
        out_specs=(hbm, hbm, hbm),
        scratch_shapes=[
            V((16, 128, 256), BF),
            V((16, 128), BF),
            V((NR, 16, 128), F32),
            V((16, 128), F32),
            V((256, 2048), BF),
            V((256, 128, 128), BF),
            dma((4,)),
            dma((16,)),
            dma((16,)),
        ],
        compiler_params=pltpu.CompilerParams(vmem_limit_bytes=60 << 20),
    )(d_bias, wp, upd, wg)
    return updated, grad_pair, grad_w.T


def solution(mesh):
    placed = (
        P(("row", "col"), None),
        P(),
        P(),
        P(("row", "col"), None),
        P(None, None, "col"),
        P("col", None),
        P("row", "col", None),
        P(),
        P(("row", "col"), None),
    )
    return jax.shard_map(
        on_device,
        mesh=mesh,
        in_specs=placed,
        out_specs=(P(("row", "col"), None), P("row", "col", None), P()),
        check_vma=False,
    )
```

```python
import jax
import jax.numpy as jnp
from jax import lax
from jax.experimental import pallas as pl
from jax.experimental.pallas import tpu as pltpu
from jax.sharding import PartitionSpec as P

MESH = pl.DeviceIdType.MESH
BF = jnp.bfloat16
F32 = jnp.float32
NC = 16
NR = 8
HD = 48
HP = 64
D = 768
DP = NC * HP
GT = 16
SCALE = 1.0 / (48.0**0.5)


def nt(a, b):
    return lax.dot_general(a, b, (((1,), (1,)), ((), ())), preferred_element_type=F32)


def nn(a, b):
    return jnp.dot(a, b, preferred_element_type=F32)


def loop(lo, hi, body):
    def step(k, carry):
        body(k)
        return carry

    lax.fori_loop(lo, hi, step, 0)


def iota(shape, dim):
    return lax.broadcasted_iota(jnp.int32, shape, dim)


def to_row(col):
    eye = iota((128, 128), 0) == iota((128, 128), 1)
    return [
        jnp.sum(jnp.where(eye, col[128 * n : 128 * n + 128], 0.0), axis=0, keepdims=True)
        for n in range(2)
    ]


def lane_sum(x):
    return jnp.broadcast_to(jnp.sum(x, axis=1, keepdims=True), x.shape)


def to_col(rows):
    eye = iota((128, 128), 0) == iota((128, 128), 1)
    return lane_sum(
        jnp.concatenate([jnp.where(eye, jnp.broadcast_to(rows[n : n + 1], (128, 128)), 0.0) for n in range(2)], axis=0)
    )


def main_kernel(
    feats, counts, w_atom, single_in, w_qkv, w_out, pair, w_pair, cot,
    d_out, upd_out, wg_out,
    pairv, feats_v, counts_v, w_atom_v, single_in_v, wt, wp_v,
    part, pool_recv, acc, norm_all, cot_all, wo_all, kv_row, kv_all, q_all, da_all,
    wbd, maskp, bias, sbuf, dpbuf, eb, st_send, st_recv, st3, mst, cst, fin3, att_send, att_recv,
    dbuf, dt, wcol, wsum, vrow, qrow, darow, single_v, upd_v,
    in_sem, pair_sem, d_sem, out_sem,
    pool_ss, pool_rs, norm_ss, norm_rs, cot_ss, cot_rs, wo_ss, wo_rs, kv_ss, kv_rs, q_ss, q_rs,
    da_ss, da_rs, st_ss, st_rs, att_ss, att_rs, wc_ss, wc_rs, kvr_ss, kvr_rs, wr_ss, wr_rs, cst_ss, cst_rs,
    fin_ss, fin_rs, mst_ss, mst_rs,
):
    r = lax.axis_index("row")
    c = lax.axis_index("col")
    chip = c // 2
    core = lax.rem(c, 2)
    mate = 2 * chip + 1 - core

    ins = [
        pltpu.make_async_copy(a, b, in_sem.at[n])
        for n, (a, b) in enumerate(
            [
                (feats, feats_v.at[pl.ds(0, 160)]),
                (counts, counts_v),
                (w_atom, w_atom_v),
                (w_pair, wp_v),
                (cot, cot_all.at[c]),
                (single_in, single_in_v),
                (w_out, wo_all.at[c, pl.ds(0, HD)]),
                (w_qkv, wt),
            ]
        )
    ]
    for cp in ins:
        cp.start()

    def pair_copy(g):
        return pltpu.make_async_copy(pair.at[pl.ds(g * GT, GT)], pairv.at[pl.ds(g * GT, GT)], pair_sem.at[g])

    loop(0, 16, lambda g: pair_copy(g).start())

    bar = pltpu.get_barrier_semaphore()

    def greet_col(k):
        pl.semaphore_signal(bar, inc=1, device_id=(r, lax.rem(c + k, NC)), device_id_type=MESH)

    def greet_row(k):
        pl.semaphore_signal(bar, inc=1, device_id=(lax.rem(r + k, NR), c), device_id_type=MESH)

    loop(1, NC, greet_col)
    loop(1, NR, greet_row)

    feats_v[160:256, :] = jnp.zeros((96, 128), BF)
    ins[1].wait()
    crow = jnp.concatenate([counts_v[pl.ds(2 * r, 1), :], counts_v[pl.ds(2 * r + 1, 1), :]], axis=1).astype(F32)
    tok = iota((256, 256), 0)
    lan = iota((256, 256), 1)
    cbig = jnp.broadcast_to(crow, (256, 256))
    ends = jnp.sum(jnp.where(lan <= tok, cbig, 0.0), axis=1, keepdims=True)
    cnt = jnp.sum(jnp.where(lan == tok, cbig, 0.0), axis=1, keepdims=True)
    atom = (lan + 160 * c).astype(F32)
    inside = jnp.logical_and(jnp.logical_and(atom < ends, atom >= ends - cnt), lan < 160)
    onehot = jnp.where(inside, 1.0, 0.0).astype(BF)
    ins[0].wait()
    ins[2].wait()
    hidden = jnp.maximum(nn(feats_v[...], w_atom_v[...]), 0.0).astype(BF)
    part[...] = (nn(onehot, hidden) / cnt).astype(BF).reshape(NC, GT, D)

    ins[3].wait()
    rep = jnp.where(iota((256, 16), 0) // 16 == iota((256, 16), 1), 1.0, 0.0).astype(BF)
    wrep = lax.dot_general(wp_v[...], rep, (((0,), (1,)), ((), ())), preferred_element_type=F32)
    lanw = lax.rem(iota((128, 256), 1), 16)
    for i in range(GT):
        wbd[128 * i : 128 * i + 128, :] = jnp.where(lanw == i, wrep, 0.0).astype(BF)
    maskp[...] = jnp.where(iota((256, DP), 1) // HP == iota((256, DP), 0) // GT, 1.0, 0.0).astype(BF)
    pad = jnp.zeros((NC, HP - HD, 256), BF)
    q_all[:, HD:HP, :] = pad
    da_all[:, HD:HP, :] = pad
    kv_all[:, 0, HD:HP, :] = pad[:, :, 0:128]
    kv_all[:, 1, HD:HP, :] = pad[:, :, 0:128]
    st_send[...] = jnp.zeros((NC, 8, 128), F32)
    wo_all[:, HD:HP, :] = jnp.zeros((NC, HP - HD, D), BF)
    for n in range(4, 8):
        ins[n].wait()

    def bias_group(k):
        gs = [2 * k, 2 * k + 1]
        for g in gs:
            pair_copy(g).wait()
        lhs = jnp.concatenate([jnp.concatenate([pairv[g * GT + i] for i in range(GT)], axis=1) for g in gs], axis=0)
        out = nn(lhs, wbd[...]).astype(BF)
        for n, g in enumerate(gs):
            bias[g] = jnp.transpose(out[128 * n : 128 * n + 128])

    loop(0, 1, bias_group)
    pl.semaphore_wait(bar, 22)

    def lo(s):
        return (160 * s) // 384

    def hi(s):
        return jnp.where(s == 15, 15, jnp.minimum(6, (160 * s + 159) // 304))

    def pool_copy(o, s):
        return pltpu.make_async_remote_copy(
            part.at[o], pool_recv.at[s], pool_ss.at[o], pool_rs.at[s], device_id=(r, o), device_id_type=MESH
        )

    def sends_to(s, o):
        return jnp.logical_and(jnp.logical_and(o >= lo(s), o <= hi(s)), o != s)

    def pool_start(o):
        @pl.when(sends_to(c, o))
        def _():
            pool_copy(o, c).start()

    loop(0, NC, pool_start)

    def piece(buf, slot, rows):
        return buf.at[slot] if rows is None else buf.at[slot, pl.ds(0, rows)]

    def gather_copy(buf, rows, ss, rs, peer, slot, n):
        return pltpu.make_async_remote_copy(
            piece(buf, slot, rows), piece(buf, slot, rows), ss.at[n], rs.at[slot], device_id=(r, peer), device_id_type=MESH
        )

    def near(k):
        return 2 * lax.rem(chip + k, 8) + core

    def gather_start(buf, rows, ss, rs):
        gather_copy(buf, rows, ss, rs, mate, c, 0).start()
        loop(1, 8, lambda k: gather_copy(buf, rows, ss, rs, near(k), c, k).start())

    def gather_relay(buf, rows, ss, rs):
        def body(k):
            slot = near(8 - k)
            gather_copy(buf, rows, ss, rs, slot, slot, k).wait_recv()
            gather_copy(buf, rows, ss, rs, mate, slot, 8 + k).start()

        loop(1, 8, body)

    def gather_end(buf, rows, ss, rs):
        def body(k):
            slot = 2 * lax.rem(chip + 8 - k, 8) + 1 - core
            gather_copy(buf, rows, ss, rs, mate, slot, 0).wait_recv()

        loop(0, 8, body)

    def gather_sent(buf, rows, ss, rs):
        def body(k):
            gather_copy(buf, rows, ss, rs, near(k), c, k).wait_send()
            gather_copy(buf, rows, ss, rs, mate, c, 8 + k).wait_send()

        gather_copy(buf, rows, ss, rs, mate, c, 0).wait_send()
        loop(1, 8, body)

    g_cot = (cot_all, None, cot_ss, cot_rs)
    g_norm = (norm_all, None, norm_ss, norm_rs)
    g_da = (da_all, HD, da_ss, da_rs)
    g_q = (q_all, HD, q_ss, q_rs)
    g_wo = (wo_all, HD, wo_ss, wo_rs)

    gather_start(*g_cot)

    loop(1, 3, bias_group)

    acc[...] = single_in_v[...].astype(F32) + part[c].astype(F32)

    def pool_take(s):
        @pl.when(sends_to(s, c))
        def _():
            pool_copy(c, s).wait_recv()
            acc[...] += pool_recv[s].astype(F32)

    loop(0, NC, pool_take)
    single = acc[...].astype(BF)
    single_v[...] = single
    v32 = single.astype(F32)
    center = jnp.mean(v32, axis=1, keepdims=True)
    diff = v32 - center
    var = jnp.mean(diff * diff, axis=1, keepdims=True)
    norm_all[c] = (diff / jnp.sqrt(var + 1e-05)).astype(BF)
    gather_start(*g_norm)

    gather_relay(*g_cot)
    loop(3, 4, bias_group)
    gather_end(*g_cot)
    da_all[c, 0:HD] = nt(wo_all[c, 0:HD], cot_all[...].reshape(256, D)).astype(BF)
    gather_start(*g_da)

    loop(4, 6, bias_group)

    gather_relay(*g_norm)
    gather_end(*g_norm)
    qkv = nt(wt[...].reshape(3 * HD, D), norm_all[...].reshape(256, D)).astype(BF)
    q_all[c, 0:HD] = qkv[0:HD]
    for half in range(2):
        for n in range(2):
            kv_row[r, half, n] = qkv[HD * (n + 1) : HD * (n + 2), 128 * half : 128 * half + 128]

    def kvr_copy(peer, slot, half):
        return pltpu.make_async_remote_copy(
            kv_row.at[slot, half],
            kv_row.at[slot, half],
            kvr_ss.at[2 * peer + half],
            kvr_rs.at[2 * slot + half],
            device_id=(peer, c),
            device_id_type=MESH,
        )

    for half in range(2):
        loop(1, NR, lambda k, half=half: kvr_copy(lax.rem(r + k, NR), r, half).start())
    gather_start(*g_q)

    def kv_copy(b, half, s):
        return pltpu.make_async_remote_copy(
            kv_row.at[b, half],
            kv_all.at[s, :, pl.ds(0, HD)],
            kv_ss.at[2 * b + half],
            kv_rs.at[s],
            device_id=(r, 2 * b + half),
            device_id_type=MESH,
        )

    def kv_forward(b, halves=(0, 1)):
        for half in halves:
            @pl.when(2 * b + half != c)
            def _(half=half):
                kv_copy(b, half, c).start()

            @pl.when(2 * b + half == c)
            def _(half=half):
                kv_all[c, :, 0:HD, :] = kv_row[b, half]

    kv_forward(r)

    def kvr_take(k, half):
        b = lax.rem(r + NR - k, NR)
        kvr_copy(b, b, half).wait_recv()
        kv_forward(b, (half,))

    for half in range(2):
        loop(1, NR, lambda k, half=half: kvr_take(k, half))
    gather_relay(*g_da)
    gather_relay(*g_q)
    loop(6, 8, bias_group)

    lan128 = iota((16, 128), 1)
    first = jnp.where(lan128 < HP, 1.0, 0.0).astype(BF)
    second = jnp.where(lan128 >= HP, 1.0, 0.0).astype(BF)
    none = jnp.zeros((16, 128), BF)

    def spread(rows_ref, m):
        out = []
        for g in range(NC):
            a, b = rows_ref[m, g, :, 0:128], rows_ref[m, g, :, 128:256]
            out += [
                jnp.concatenate([a * first, none], axis=1),
                jnp.concatenate([a * second, none], axis=1),
                jnp.concatenate([none, b * first], axis=1),
                jnp.concatenate([none, b * second], axis=1),
            ]
        return jnp.concatenate(out, axis=0)

    def head_ready(h):
        @pl.when(h != c)
        def _():
            kv_copy(0, 0, h).wait_recv()

        @pl.when(jnp.logical_and(lax.rem(h, 2) != core, h != c))
        def _():
            gather_copy(*g_q, mate, h, 0).wait_recv()
            gather_copy(*g_da, mate, h, 0).wait_recv()

    def quad(m):
        loop(4 * m, 4 * m + 4, head_ready)
        qrow[m] = jnp.transpose(q_all[4 * m : 4 * m + 4].reshape(256, 256)).reshape(NC, GT, 256)
        darow[m] = jnp.transpose(da_all[4 * m : 4 * m + 4].reshape(256, 256)).reshape(NC, GT, 256)
        kt = kv_all[4 * m : 4 * m + 4, 0].reshape(4 * HP, 128)
        vt = kv_all[4 * m : 4 * m + 4, 1].reshape(4 * HP, 128)
        sbuf[m] = nn(spread(qrow, m), kt).reshape(NC, 64, 128)
        dpbuf[m] = nn(spread(darow, m), vt).reshape(NC, 64, 128)
        vrow[2 * m] = jnp.transpose(vt[0:128])
        vrow[2 * m + 1] = jnp.transpose(vt[128:256])

    for m in range(4):
        quad(m)
    gather_start(*g_wo)

    def st_copy(g, s):
        return pltpu.make_async_remote_copy(
            st_send.at[g], st_recv.at[s], st_ss.at[g], st_rs.at[s], device_id=(r, g), device_id_type=MESH
        )

    U = 4

    def soft_step(q):
        gs = [U * q + u for u in range(U)]
        s = jnp.concatenate([sbuf[m, g] for g in gs for m in range(4)], axis=0)
        b = jnp.concatenate([bias[g] for g in gs], axis=0)
        dp = jnp.concatenate([dpbuf[m, g] for g in gs for m in range(4)], axis=0)
        s = s * SCALE + b.astype(F32)
        top = jnp.max(s, axis=1, keepdims=True)
        e = jnp.exp(s - top)
        l = lane_sum(e)
        t = lane_sum(e * dp)
        e16 = e.astype(BF)
        top = jnp.broadcast_to(top, e.shape)
        stats = [
            jnp.concatenate([row for u in range(U) for row in to_row(x[256 * u : 256 * u + 256])], axis=0)
            for x in (top, l, t)
        ]
        for u, g in enumerate(gs):
            for m in range(4):
                k = 256 * u + 64 * m
                sbuf[m, g] = e[k : k + 64]
                eb[m, g] = e16[k : k + 64]
            st_send[g, 0:2] = stats[0][2 * u : 2 * u + 2]
        for n in range(3):
            st3[n, pl.ds(2 * U * q, 2 * U)] = stats[n]

    loop(0, 2, lambda n: soft_step(2 * (1 - core) + n))

    def half_of(ref, k):
        return ref.at[:, pl.ds(16 * k, 16)]

    half_copy = pltpu.make_async_remote_copy(
        half_of(st3, 1 - core), mst, mst_ss, mst_rs, device_id=(r, mate), device_id_type=MESH
    )
    half_copy.start()
    loop(0, 2, lambda n: soft_step(2 * core + n))

    def att_copy(g, s):
        return pltpu.make_async_remote_copy(
            att_send.at[g], att_recv.at[s], att_ss.at[g], att_rs.at[s], device_id=(r, g), device_id_type=MESH
        )

    half_copy.wait_recv()
    sa, sb = st3[:, pl.ds(16 * core, 16)], mst[...]
    top2 = jnp.maximum(sa[0], sb[0])
    fa, fb = jnp.exp(sa[0] - top2), jnp.exp(sb[0] - top2)
    cst[chip, 0] = top2
    cst[chip, 1] = sa[1] * fa + sb[1] * fb
    cst[chip, 2] = sa[2] * fa + sb[2] * fb

    def cst_copy(peer, slot):
        return pltpu.make_async_remote_copy(
            cst.at[slot], cst.at[slot], cst_ss.at[peer], cst_rs.at[slot], device_id=(r, 2 * peer + core), device_id_type=MESH
        )

    loop(1, 8, lambda k: cst_copy(lax.rem(chip + k, 8), chip).start())
    keep = iota((16, 16, 128), 2) < HP
    for p in range(8):
        rows = eb[p // 2, :, 32 * (p % 2) : 32 * (p % 2) + 32, :].reshape(512, 128)
        full = nn(rows, vrow[p]).reshape(NC, 2, GT, 128)
        att_send[:, :, 128 * p : 128 * p + 128] = jnp.where(keep, full[:, 0], full[:, 1]).astype(BF)

    def att_start(k):
        g = lax.rem(c + k, NC)
        st_copy(g, c).start()
        att_copy(g, c).start()

    loop(1, NC, att_start)
    st_recv[c] = st_send[c]
    att_recv[c] = att_send[c]
    loop(1, 8, lambda k: cst_copy(chip, lax.rem(chip + 8 - k, 8)).wait_recv())
    all_st = cst[...]
    best = jnp.max(all_st[:, 0], axis=0)
    fac = jnp.exp(all_st[:, 0] - best[None])
    inv = 1.0 / jnp.sum(fac * all_st[:, 1], axis=0)
    mine = pl.ds(16 * core, 16)
    fin3[0, mine] = best
    fin3[1, mine] = inv
    fin3[2, mine] = jnp.sum(fac * all_st[:, 2], axis=0) * inv

    def fin_copy(k):
        return pltpu.make_async_remote_copy(
            half_of(fin3, k), half_of(fin3, k), fin_ss, fin_rs, device_id=(r, mate), device_id_type=MESH
        )

    fin_copy(core).start()


    def d_copy(g):
        return pltpu.make_async_copy(dt.at[g], d_out.at[g], d_sem.at[g])

    W = 8

    def d_step(n):
        k = lax.rem(core + n, 2)

        @pl.when(n == 1)
        def _():
            fin_copy(1 - core).wait_recv()

        half = pl.ds(16 * k, 16)
        scales = jnp.exp(st3[0, half] - fin3[0, half]) * fin3[1, half]
        inners = fin3[2, half]
        scale = [to_col(scales[2 * u : 2 * u + 2]) for u in range(W)]
        inner = [to_col(inners[2 * u : 2 * u + 2]) for u in range(W)]
        gs = [W * k + u for u in range(W)]
        e = jnp.concatenate([sbuf[m, g] for g in gs for m in range(4)], axis=0)
        dp = jnp.concatenate([dpbuf[m, g] for g in gs for m in range(4)], axis=0)
        d = (e * jnp.concatenate(scale, axis=0)) * (dp - jnp.concatenate(inner, axis=0))
        dbuf[pl.ds(W * k, W)] = d.reshape(W, 256, 128)

    loop(0, 2, d_step)

    def weight_step(q):
        lhs = [dbuf[4 * q + n, pl.ds(i, NC, stride=GT), :] for n in range(4) for i in range(GT)]
        rhs = pairv[pl.ds(4 * GT * q, 4 * GT)].reshape(4 * GT * 128, 128)
        return nn(jnp.concatenate(lhs, axis=1).astype(BF), rhs)

    wcol[c] = lax.fori_loop(0, 4, lambda q, tot: tot + weight_step(q), jnp.zeros((16, 128), F32))

    def wc_copy(peer, slot):
        return pltpu.make_async_remote_copy(
            wcol.at[slot], wcol.at[slot], wc_ss.at[peer], wc_rs.at[slot], device_id=(r, peer), device_id_type=MESH
        )

    loop(1, NC, lambda k: wc_copy(lax.rem(c + k, NC), c).start())

    gather_relay(*g_wo)

    def d_turn(g):
        dt[g] = jnp.transpose(dbuf[g].astype(BF))
        d_copy(g).start()

    loop(0, 16, d_turn)

    loop(1, NC, lambda k: wc_copy(c, lax.rem(c + NC - k, NC)).wait_recv())
    wsum[...] = jnp.sum(wcol[...], axis=0)

    def wr_copy(peer, slot):
        return pltpu.make_async_remote_copy(
            wsum, wg_out.at[slot], wr_ss.at[peer], wr_rs.at[slot], device_id=(peer, c), device_id_type=MESH
        )

    loop(1, NR, lambda k: wr_copy(lax.rem(r + k, NR), r).start())
    wg_copy = pltpu.make_async_copy(wsum, wg_out.at[r], out_sem.at[1])
    wg_copy.start()

    def att_take(k):
        s = lax.rem(c + NC - k, NC)
        st_copy(c, s).wait_recv()
        att_copy(c, s).wait_recv()

    loop(1, NC, att_take)
    here = pl.ds(2 * c, 2)
    frow = jnp.exp(st_recv[:, 0:2, :] - fin3[0, here][None]) * fin3[1, here][None]
    fwide = jnp.concatenate([frow[:, 0, :], frow[:, 1, :]], axis=1)
    fbig = jnp.broadcast_to(fwide[:, None, :], (16, 16, 256))
    diag = lax.rem(iota((16, 16, 256), 2), 16) == iota((16, 16, 256), 1)
    fbig = jnp.where(diag, fbig, 0.0).reshape(256, 256)
    f_hi = fbig.astype(BF)
    f_lo = (fbig - f_hi.astype(F32)).astype(BF)
    f_all = (nn(f_hi, maskp[...]) + nn(f_lo, maskp[...])).reshape(16, 16, DP)
    att = jnp.sum(att_recv[...].astype(F32) * f_all, axis=0).astype(BF)
    gather_end(*g_wo)
    proj = nn(att, wo_all[...].reshape(DP, D))
    upd_v[...] = (single_v[...].astype(F32) + proj).astype(BF)
    upd_copy = pltpu.make_async_copy(upd_v, upd_out, out_sem.at[0])
    upd_copy.start()

    def pool_sent(o):
        @pl.when(sends_to(c, o))
        def _():
            pool_copy(o, c).wait_send()

    loop(0, NC, pool_sent)
    for g in (g_cot, g_norm, g_da, g_q, g_wo):
        gather_sent(*g)
    for half in range(2):
        loop(1, NR, lambda k, half=half: kvr_copy(lax.rem(r + k, NR), r, half).wait_send())

    def kv_sent(b):
        for half in range(2):
            @pl.when(2 * b + half != c)
            def _(half=half):
                kv_copy(b, half, c).wait_send()

    loop(0, NR, kv_sent)

    def col_sent(k):
        p = lax.rem(c + k, NC)
        st_copy(p, c).wait_send()
        att_copy(p, c).wait_send()
        wc_copy(p, c).wait_send()

    loop(1, NC, col_sent)
    half_copy.wait_send()
    fin_copy(core).wait_send()
    loop(1, 8, lambda k: cst_copy(lax.rem(chip + k, 8), chip).wait_send())
    loop(0, 16, lambda g: d_copy(g).wait())
    upd_copy.wait()
    loop(1, NR, lambda k: wr_copy(r, lax.rem(r + NR - k, NR)).wait_recv())
    loop(1, NR, lambda k: wr_copy(lax.rem(r + k, NR), r).wait_send())
    wg_copy.wait()


def grad_kernel(d, w_pair, upd, wg, upd_out, grad, wg_out, dv, wp_v, wr_v, wg_v, w2, out, in_sem, d_sem, sem):
    small = [
        pltpu.make_async_copy(w_pair, wp_v, in_sem.at[0]),
        pltpu.make_async_copy(upd, upd_out, in_sem.at[1]),
        pltpu.make_async_copy(wg, wr_v, in_sem.at[2]),
    ]
    for cp in small:
        cp.start()

    def d_copy(g):
        return pltpu.make_async_copy(d.at[g], dv.at[g], d_sem.at[g])

    loop(0, 16, lambda g: d_copy(g).start())
    rep = jnp.where(iota((256, 16), 0) // 16 == iota((256, 16), 1), 1.0, 0.0).astype(BF)
    small[0].wait()
    wrep = nn(rep, wp_v[...])
    rowm = lax.rem(iota((256, 128), 0), 16)
    for i in range(GT):
        w2[:, 128 * i : 128 * i + 128] = jnp.where(rowm == i, wrep, 0.0).astype(BF)

    def copy(g):
        return pltpu.make_async_copy(out.at[pl.ds(g * GT, GT)], grad.at[pl.ds(g * GT, GT)], sem.at[g])

    def step(g):
        d_copy(2 * g).wait()
        d_copy(2 * g + 1).wait()
        lhs = dv[pl.ds(2 * g, 2)].reshape(256, 256)
        for n in range(8):
            full = nn(lhs, w2[:, 256 * n : 256 * n + 256]).astype(BF)
            for k in range(2):
                for i in range(2):
                    out[(2 * g + k) * GT + 2 * n + i] = full[128 * k : 128 * k + 128, 128 * i : 128 * i + 128]
        copy(2 * g).start()
        copy(2 * g + 1).start()

    loop(0, 8, step)
    small[2].wait()
    wg_v[...] = jnp.sum(wr_v[...], axis=0)
    wg_copy = pltpu.make_async_copy(wg_v, wg_out, in_sem.at[3])
    wg_copy.start()
    loop(0, 16, lambda g: copy(g).wait())
    small[1].wait()
    wg_copy.wait()


def on_device(atom_feats, atom_counts, w_atom, single_in, w_qkv, w_out, pair, w_pair, cotangent):
    hbm = pl.BlockSpec(memory_space=pl.ANY)
    V = pltpu.VMEM
    dma = pltpu.SemaphoreType.DMA
    wp = w_pair.T
    d_bias, upd, wg = pl.pallas_call(
        main_kernel,
        name="attend",
        out_shape=(
            jax.ShapeDtypeStruct((16, 128, 256), BF),
            jax.ShapeDtypeStruct((16, D), BF),
            jax.ShapeDtypeStruct((NR, 16, 128), F32),
        ),
        in_specs=[hbm] * 9,
        out_specs=(hbm, hbm, hbm),
        scratch_shapes=[
            V((256, 128, 128), BF),
            V((256, 128), BF),
            V((16, 128), jnp.int32),
            V((128, D), BF),
            V((16, D), BF),
            V((3, HD, D), BF),
            V((16, 128), BF),
            V((16, 16, D), BF),
            V((16, 16, D), BF),
            V((16, D), F32),
            V((16, 16, D), BF),
            V((16, 16, D), BF),
            V((16, HP, D), BF),
            V((8, 2, 2, HD, 128), BF),
            V((16, 2, HP, 128), BF),
            V((16, HP, 256), BF),
            V((16, HP, 256), BF),
            V((2048, 256), BF),
            V((256, DP), BF),
            V((16, 256, 128), BF),
            V((4, 16, 64, 128), F32),
            V((4, 16, 64, 128), F32),
            V((4, 16, 64, 128), BF),
            V((16, 8, 128), F32),
            V((16, 8, 128), F32),
            V((3, 32, 128), F32),
            V((3, 16, 128), F32),
            V((8, 3, 16, 128), F32),
            V((3, 32, 128), F32),
            V((16, 16, DP), BF),
            V((16, 16, DP), BF),
            V((16, 256, 128), F32),
            V((16, 128, 256), BF),
            V((16, 16, 128), F32),
            V((16, 128), F32),
            V((8, 128, 128), BF),
            V((4, 16, 16, 256), BF),
            V((4, 16, 16, 256), BF),
            V((16, D), BF),
            V((16, D), BF),
            dma((8,)),
            dma((16,)),
            dma((16,)),
            dma((2,)),
        ]
        + [dma((16,))] * 22
        + [dma((8,))] * 4
        + [dma] * 4,
        compiler_params=pltpu.CompilerParams(collective_id=0, has_side_effects=True, vmem_limit_bytes=56 << 20),
    )(
        atom_feats,
        atom_counts.reshape(16, 128),
        w_atom,
        single_in,
        jnp.swapaxes(w_qkv, 1, 2),
        w_out,
        pair,
        wp,
        cotangent,
    )
    updated, grad_pair, grad_w = pl.pallas_call(
        grad_kernel,
        name="grad_pair",
        out_shape=(
            jax.ShapeDtypeStruct((16, D), BF),
            jax.ShapeDtypeStruct((256, 128, 128), BF),
            jax.ShapeDtypeStruct((16, 128), F32),
        ),
        in_specs=[hbm] * 4,
        out_specs=(hbm, hbm, hbm),
        scratch_shapes=[
            V((16, 128, 256), BF),
            V((16, 128), BF),
            V((NR, 16, 128), F32),
            V((16, 128), F32),
            V((256, 2048), BF),
            V((256, 128, 128), BF),
            dma((4,)),
            dma((16,)),
            dma((16,)),
        ],
        compiler_params=pltpu.CompilerParams(vmem_limit_bytes=60 << 20),
    )(d_bias, wp, upd, wg)
    return updated, grad_pair, grad_w.T


def solution(mesh):
    placed = (
        P(("row", "col"), None),
        P(),
        P(),
        P(("row", "col"), None),
        P(None, None, "col"),
        P("col", None),
        P("row", "col", None),
        P(),
        P(("row", "col"), None),
    )
    return jax.shard_map(
        on_device,
        mesh=mesh,
        in_specs=placed,
        out_specs=(P(("row", "col"), None), P("row", "col", None), P()),
        check_vma=False,
    )
```
